32 devices in a mesh: grp: 4 (over y, x), seq: 8 (over z, core).
Axes of the slice: x: 2, y: 2, z: 4, core: 2. Of those that a mesh axis runs over, the one named last changes fastest.
Arguments:
- lin_q: bfloat16 [2048, 8192], P('seq', 'grp'), may hold values from -6 to 6
- lin_k: bfloat16 [2048, 8192], P('seq', 'grp'), may hold values from -6 to 6
- lin_v: bfloat16 [2048, 8192], P('seq', 'grp'), may hold values from -60 to 60
- lin_gain: float32 [8192], P('grp'), may hold values from 0.1 to 1.9
- soft_q: bfloat16 [2048, 8192], P('seq', 'grp'), may hold values from -6 to 6
- soft_k: bfloat16 [2048, 8192], P('seq', 'grp'), may hold values from -12.5 to 12.5
- soft_v: bfloat16 [2048, 8192], P('seq', 'grp'), may hold values from -6 to 6
Outputs:
- lin_out: bfloat16 [2048, 8192], P('seq', 'grp')
- soft_out: bfloat16 [2048, 8192], P('seq', 'grp')
The draws below stay inside these ranges and needn't reach their ends.
All inputs are finite; a program needn't handle non-finite values.
Results may differ from the reference program's by a relative error of at most 0.0031.
Values may be sent and summed in bfloat16 or wider, within the bound.
No kernel may reach another device: no remote copies, remote signals or barrier semaphores. Data moves between devices by JAX's collectives and lax.ppermute only.
A program may use at most 192 MiB of HBM per device.

```python
import jax
import jax.numpy as jnp
from jax import lax

HEADS = 64
HEAD_DIM = 128
TOK_DEV = 256
SEQ_LEN = 2048
WIDTH = 8192
N_SEQ = 8


def soft_pair(key):
    base_key = jax.random.fold_in(key, 7)
    key_query, key_keys = jax.random.split(base_key, 2)
    seq_len = TOK_DEV * N_SEQ
    full_width = HEADS * HEAD_DIM
    shape_full = (seq_len, full_width)
    queries = jnp.clip(jax.random.normal(key_query, shape_full, jnp.float32), -6.0, 6.0)
    keys_all = 2.5 * jnp.clip(jax.random.normal(key_keys, shape_full, jnp.float32), -5.0, 5.0)
    return (queries, keys_all)


def draw_soft_q(key, part):
    return soft_pair(key)[0].astype(jnp.bfloat16)


def draw_soft_k(key, part):
    return soft_pair(key)[1].astype(jnp.bfloat16)


def draw_lin_v(key, part):
    seq_len = TOK_DEV * N_SEQ
    full_width = HEADS * HEAD_DIM
    value_key = jax.random.fold_in(key, 11)
    levels = (jnp.arange(full_width) // HEAD_DIM).astype(jnp.float32) / (HEADS - 1)
    base_draw = jnp.clip(jax.random.normal(value_key, (seq_len, full_width), jnp.float32), -6.0, 6.0)
    column_scale = jnp.power(10.0, levels)
    return (base_draw * column_scale[None, :]).astype(jnp.bfloat16)


def shard_levels(own_key, shape, shards, smallest, high):
    level, own = 1.0, jax.random.fold_in(own_key, 6)
    for axis_at, blocks in shards:
        heights = jnp.exp(jax.random.uniform(jax.random.fold_in(own, axis_at), (blocks,), jnp.float32, smallest / len(shards), high / len(shards)))
        level = level * jnp.repeat(heights, shape[axis_at] // blocks).reshape([-1 if axis == axis_at else 1 for axis in range(len(shape))])
    return level


def centred(rng, shape, deviation, bound, shards=(), kind=jnp.bfloat16):
    loudness = shard_levels(rng, shape, shards, -0.22, 0.18) if shards else 1.0
    result = jax.random.normal(rng, shape, jnp.float32) * deviation * loudness
    return jnp.minimum(jnp.maximum(result, -bound), bound).astype(kind)


def setup_inputs(seed: int = 0) -> dict:
    key_of = jax.random.split(jax.random.key(seed), 8)
    lin_q = centred(key_of[0], (SEQ_LEN, WIDTH), 1.0, 6.0, ((0, 8), (1, 4)))
    lin_k = centred(key_of[1], (SEQ_LEN, WIDTH), 1.0, 6.0, ((0, 8), (1, 4)))
    lin_v = draw_lin_v(jax.random.fold_in(key_of[7], 71), 0)
    lin_gain = jnp.clip(1.0 + 0.18 * jax.random.normal(key_of[3], (WIDTH,), jnp.float32), 0.1, 1.9)
    soft_q = draw_soft_q(jax.random.fold_in(key_of[7], 71), 0)
    soft_k = draw_soft_k(jax.random.fold_in(key_of[7], 71), 0)
    soft_v = centred(key_of[6], (SEQ_LEN, WIDTH), 1.0, 6.0, ((0, 8), (1, 4)))
    return dict(lin_q=lin_q, lin_k=lin_k, lin_v=lin_v, lin_gain=lin_gain, soft_q=soft_q, soft_k=soft_k, soft_v=soft_v)


highest = lax.Precision.HIGHEST
epsilon = 1e-06

def reference(lin_q, lin_k, lin_v, lin_gain, soft_q, soft_k, soft_v):
    seq_len = TOK_DEV * N_SEQ
    full_width = HEADS * HEAD_DIM

    def split_blocks(source):
        return source.astype(jnp.float32).reshape(N_SEQ, TOK_DEV, HEADS, HEAD_DIM)
    causal = jnp.tril(jnp.ones((TOK_DEV, TOK_DEV), jnp.float32))

    def block_step(memory, inputs):
        queries, keys_block, values = inputs
        carried = jnp.einsum('thd,hde->the', queries, memory, precision=highest)
        scores = jnp.einsum('thd,shd->hts', queries, keys_block, precision=highest) * causal[None]
        within = jnp.einsum('hts,she->the', scores, values, precision=highest)
        own_state = jnp.einsum('thd,the->hde', keys_block, values, precision=highest)
        return (memory + own_state, within + carried)
    initial = jnp.zeros((HEADS, HEAD_DIM, HEAD_DIM), jnp.float32)
    final_state, mixed_out = lax.scan(block_step, initial, (split_blocks(lin_q), split_blocks(lin_k), split_blocks(lin_v)))
    mixed_out = mixed_out.reshape(seq_len, full_width)
    squares = lax.optimization_barrier(jnp.sum(mixed_out * mixed_out, axis=1))
    inverse = lax.rsqrt(squares / full_width + epsilon)
    lin_out = (mixed_out * inverse[:, None] * lin_gain).astype(jnp.bfloat16)
    scale = HEAD_DIM ** (-0.5)

    def one_head(operands):
        head_q, head_k, head_v = operands
        block_rows = min(512, seq_len)
        pieces = []
        for block_index in range(seq_len // block_rows):
            first_row = block_index * block_rows
            last_row = first_row + block_rows
            scores = jnp.dot(head_q[first_row:last_row], head_k[:last_row].T, preferred_element_type=jnp.float32) * scale
            positions_q = first_row + jnp.arange(block_rows)[:, None]
            positions_k = jnp.arange(last_row)[None, :]
            scores = jnp.where(positions_k <= positions_q, scores, -1e+30)
            largest = lax.optimization_barrier(jnp.max(scores, axis=1, keepdims=True))
            exponent = jnp.exp(scores - largest)
            denominator = lax.optimization_barrier(jnp.sum(exponent, axis=1, keepdims=True))
            weights = exponent.astype(jnp.bfloat16)
            numerator = jnp.dot(weights, head_v[:last_row], preferred_element_type=jnp.float32)
            pieces.append((numerator / denominator).astype(jnp.bfloat16))
        return jnp.concatenate(pieces, axis=0)

    def by_heads(source):
        return source.reshape(seq_len, HEADS, HEAD_DIM).transpose(1, 0, 2)
    heads_out = lax.map(one_head, (by_heads(soft_q), by_heads(soft_k), by_heads(soft_v)))
    soft_out = heads_out.transpose(1, 0, 2).reshape(seq_len, full_width)
    return (lin_out, soft_out)
```

```python
import functools

import jax
import jax.numpy as jnp
from jax import lax
from jax.experimental import pallas as pl
from jax.experimental.pallas import tpu as pltpu
from jax.sharding import PartitionSpec as P

HEADS = 64
HEAD_DIM = 128
LSE_ROWS = 16
CHUNKS = (4, 4, 4, 4)
STEP = 4

highest = lax.Precision.HIGHEST
epsilon = 1e-06
F32 = jnp.float32
BF16 = jnp.bfloat16
LOG2 = HEAD_DIM ** (-0.5) * 1.4426950408889634
NT = (((1,), (1,)), ((), ()))
TN = (((0,), (0,)), ((), ()))


def dot_nt(a, b):
    return lax.dot_general(a, b, NT, preferred_element_type=F32)


def dot_tn(a, b):
    return lax.dot_general(a, b, TN, preferred_element_type=F32)


def dot(a, b):
    return jnp.dot(a, b, preferred_element_type=F32)


def split(a):
    high = a.astype(BF16)
    return high, (a - high.astype(F32)).astype(BF16)


def after(value, *others):
    return lax.optimization_barrier((value, *others))[0]


def causal_mask(rows):
    row_ids = lax.broadcasted_iota(jnp.int32, (rows, rows), 0)
    col_ids = lax.broadcasted_iota(jnp.int32, (rows, rows), 1)
    return col_ids <= row_ids


def lanes(ref, head):
    return ref[:, head * HEAD_DIM : (head + 1) * HEAD_DIM]


def weigh(scores, values, top):
    both = None
    for score, value in zip(scores, values):
        weights = jnp.exp2(score * LOG2 - top).astype(BF16)
        part = dot(weights, jnp.concatenate([value, jnp.ones_like(value)], axis=1))
        both = part if both is None else both + part
    return both[:, :HEAD_DIM], both[:, HEAD_DIM:]


def partial_attention(query, keys, values):
    rows = query.shape[0]
    scores = [dot_nt(query, key) for key in keys]
    top = jnp.max(functools.reduce(jnp.maximum, scores), axis=1, keepdims=True) * LOG2
    numerator, total = weigh(scores, values, top)
    across = jnp.transpose(top + jnp.log2(total))[:1]
    parts = []
    for _ in range(3):
        part = across.astype(BF16).astype(F32)
        across = across - part
        parts += [part[:, i : i + HEAD_DIM] for i in range(0, rows, HEAD_DIM)]
    parts.append(jnp.zeros((LSE_ROWS - len(parts), HEAD_DIM), F32))
    return jnp.concatenate([numerator * (1.0 / total)] + parts, axis=0).astype(BF16)


def read_partial(packed, rows):
    halves = rows // HEAD_DIM
    level = packed[rows:].astype(F32)
    columns = []
    for i in range(halves):
        line = level[i : i + 1] + level[halves + i : halves + i + 1] + level[2 * halves + i : 2 * halves + i + 1]
        columns.append(jnp.transpose(jnp.broadcast_to(line, (HEAD_DIM, HEAD_DIM))))
    return packed[:rows].astype(F32), jnp.concatenate(columns, axis=0)


def serve_kernel(place, first_ref, second_ref, own_ref, sib_ref, far_ref, farx_ref, out1_ref, out2_ref):
    rows, width = first_ref.shape
    chip = place[0]

    def attend(query_ref, key_refs, out_ref):
        for head in range(width // HEAD_DIM):
            both = [lanes(ref, head) for ref in key_refs]
            packed = partial_attention(lanes(query_ref, head), [b[:rows] for b in both], [b[rows:] for b in both])
            out_ref[:, head * HEAD_DIM : (head + 1) * HEAD_DIM] = packed

    @pl.when(chip == 1)
    def _():
        attend(first_ref, [far_ref, farx_ref, own_ref, sib_ref], out1_ref)
        attend(second_ref, [far_ref, farx_ref, own_ref, sib_ref], out2_ref)

    @pl.when(chip == 2)
    def _():
        attend(first_ref, [own_ref, sib_ref], out1_ref)


def finish_kernel(place, query_ref, own_ref, sib_ref, far_ref, farx_ref, part1_ref, part2_ref, *out_refs):
    out_ref = out_refs[-1]
    chip, core = place[0], place[1]
    rows, width = query_ref.shape
    mask = causal_mask(rows)

    def attend(whole, partials):
        for head in range(width // HEAD_DIM):
            query = lanes(query_ref, head)
            both = [lanes(ref, head) for ref in [own_ref, sib_ref] + whole]
            scores = [dot_nt(query, b[:rows]) for b in both]
            scores[0] = jnp.where(mask, scores[0], -1e30)
            scores[1] = jnp.where(core == 1, scores[1], -1e30)
            top = jnp.max(functools.reduce(jnp.maximum, scores), axis=1, keepdims=True) * LOG2
            terms = [read_partial(lanes(ref, head), rows) for ref in partials]
            for _, level in terms:
                top = jnp.maximum(top, level)
            numerator, total = weigh(scores, [b[rows:] for b in both], top[:, :1])
            for normalized, level in terms:
                weight = jnp.exp2(level - top)
                total = total + weight
                numerator = numerator + weight * normalized
            out_ref[:, head * HEAD_DIM : (head + 1) * HEAD_DIM] = (numerator / total).astype(BF16)

    @pl.when(chip == 0)
    def _():
        attend([], [])

    @pl.when(chip == 1)
    def _():
        attend([far_ref, farx_ref], [])

    @pl.when(chip == 2)
    def _():
        attend([], [part1_ref])

    @pl.when(chip == 3)
    def _():
        attend([], [part1_ref, part2_ref])


def col_block(rows, step, offset=0):
    return pl.BlockSpec((rows, step * HEAD_DIM), lambda h: (0, offset // step + h))


SMEM_SPEC = pl.BlockSpec(memory_space=pltpu.SMEM)


def params():
    return pltpu.CompilerParams(vmem_limit_bytes=40 * 1024 * 1024)


def tiny():
    return pl.CostEstimate(flops=1, bytes_accessed=1, transcendentals=0)


def serve(place, first, second, own, sib, far, farx, offset):
    rows, width = first.shape
    step = min(STEP, width // HEAD_DIM)
    sent = jax.ShapeDtypeStruct((rows + LSE_ROWS, width), BF16)
    kv = col_block(2 * rows, step)
    kv_at = col_block(2 * rows, step, offset)
    out = col_block(rows + LSE_ROWS, step)
    return pl.pallas_call(
        serve_kernel,
        grid=(width // HEAD_DIM // step,),
        out_shape=(sent, sent),
        in_specs=[SMEM_SPEC, col_block(rows, step), col_block(rows, step), kv_at, kv_at, kv, kv],
        out_specs=(out, out),
        compiler_params=params(),
        cost_estimate=tiny(),
        name="serve",
    )(place, first, second, own, sib, far, farx)


def finish(place, query, own, sib, far, farx, part1, part2, out, offset):
    rows = query.shape[0]
    width = part1.shape[1]
    step = min(STEP, width // HEAD_DIM)
    kv = col_block(2 * rows, step)
    kv_at = col_block(2 * rows, step, offset)
    part = col_block(rows + LSE_ROWS, step)
    earlier = () if out is None else (out,)
    return pl.pallas_call(
        finish_kernel,
        grid=(width // HEAD_DIM // step,),
        out_shape=jax.ShapeDtypeStruct(query.shape, BF16),
        in_specs=[SMEM_SPEC, col_block(rows, step, offset), kv_at, kv_at, kv, kv, part, part] + [pl.BlockSpec(memory_space=pl.ANY)] * len(earlier),
        out_specs=col_block(rows, step, offset),
        input_output_aliases={8: 0} if earlier else {},
        compiler_params=params(),
        cost_estimate=tiny(),
        name="finish",
    )(place, query, own, sib, far, farx, part1, part2, *earlier)


def state_kernel(key_ref, value_ref, state_ref):
    for head in range(state_ref.shape[0]):
        state_ref[head] = dot_tn(lanes(key_ref, head), lanes(value_ref, head))


def own_states(keys, values):
    rows, width = keys.shape
    heads = width // HEAD_DIM
    return pl.pallas_call(
        state_kernel,
        grid=(heads // STEP,),
        out_shape=jax.ShapeDtypeStruct((heads, HEAD_DIM, HEAD_DIM), F32),
        in_specs=[col_block(rows, STEP), col_block(rows, STEP)],
        out_specs=pl.BlockSpec((STEP, HEAD_DIM, HEAD_DIM), lambda h: (h, 0, 0)),
        compiler_params=params(),
        cost_estimate=tiny(),
        name="states",
    )(keys, values)


def mix_kernel(place, query_ref, key_ref, value_ref, before_ref, sib_ref, mixed_ref, square_ref):
    rows, width = query_ref.shape
    mask = causal_mask(rows)
    squares = jnp.zeros((rows, HEAD_DIM), F32)
    for head in range(width // HEAD_DIM):
        query, value = lanes(query_ref, head), lanes(value_ref, head)
        high, low = split(jnp.where(mask, dot_nt(query, lanes(key_ref, head)), 0.0))
        prefix = before_ref[head].astype(F32) + jnp.where(place[1] == 1, sib_ref[head], 0.0)
        prefix_high, prefix_low = split(prefix)
        mixed = dot(high, value) + dot(low, value) + dot(query, prefix_high) + dot(query, prefix_low)
        mixed_ref[:, head * HEAD_DIM : (head + 1) * HEAD_DIM] = mixed
        squares = squares + mixed * mixed

    @pl.when(pl.program_id(0) == 0)
    def _():
        square_ref[...] = squares

    @pl.when(pl.program_id(0) > 0)
    def _():
        square_ref[...] += squares


def mix(place, queries, keys, values, before, sib_state):
    rows, width = keys.shape
    heads = width // HEAD_DIM
    state_block = pl.BlockSpec((STEP, HEAD_DIM, HEAD_DIM), lambda h: (h, 0, 0))
    return pl.pallas_call(
        mix_kernel,
        grid=(heads // STEP,),
        out_shape=(jax.ShapeDtypeStruct((rows, width), F32), jax.ShapeDtypeStruct((rows, HEAD_DIM), F32)),
        in_specs=[SMEM_SPEC, col_block(rows, STEP), col_block(rows, STEP), col_block(rows, STEP), state_block, state_block],
        out_specs=(col_block(rows, STEP), pl.BlockSpec((rows, HEAD_DIM), lambda h: (0, 0))),
        compiler_params=params(),
        cost_estimate=tiny(),
        name="mix",
    )(place, queries, keys, values, before, sib_state)


def from_behind(value, axis, by):
    peers = lax.axis_size(axis)
    pairs = [(i, i + by) for i in range(peers) if 0 <= i + by < peers]
    return lax.ppermute(value, axis, pairs)


def any_ring(lin_q, lin_k, lin_v, lin_gain, soft_q, soft_k, soft_v):
    rows_dev, width_dev = lin_q.shape
    head_size = HEAD_DIM
    local_heads = width_dev // head_size
    queries_low = lin_q.reshape(rows_dev, local_heads, head_size)
    keys_low = lin_k.reshape(rows_dev, local_heads, head_size)
    values_low = lin_v.reshape(rows_dev, local_heads, head_size)
    queries = queries_low.astype(jnp.float32)
    values_lin = values_low.astype(jnp.float32)
    own_state = jnp.einsum("thd,the->hde", keys_low, values_low, preferred_element_type=jnp.float32)
    zero_state = jnp.zeros_like(own_state)

    def relay_step(counter, running):
        return from_behind(running + own_state, "seq", 1)

    prefix = lax.fori_loop(0, lax.axis_size("seq") - 1, relay_step, zero_state)
    row_ids = lax.broadcasted_iota(jnp.int32, (rows_dev, rows_dev), 0)
    col_ids = lax.broadcasted_iota(jnp.int32, (rows_dev, rows_dev), 1)
    causal = (col_ids <= row_ids).astype(jnp.float32)
    scores_lin = (
        jnp.einsum("thd,shd->hts", queries_low, keys_low, preferred_element_type=jnp.float32)
        * causal[None]
    )
    within = jnp.einsum("hts,she->the", scores_lin, values_lin, precision=highest)
    carried = jnp.einsum("thd,hde->the", queries, prefix, precision=highest)
    mixed_out = (within + carried).reshape(rows_dev, width_dev)
    squares = jnp.sum(mixed_out * mixed_out, axis=1)
    summed = lax.psum(squares, "grp")
    inverse = lax.rsqrt(summed / (HEADS * head_size) + epsilon)
    lin_out = (mixed_out * inverse[:, None] * lin_gain).astype(jnp.bfloat16)
    seq_devices = lax.axis_size("seq")
    seq_index = lax.axis_index("seq")
    units = 2 * local_heads // seq_devices
    half_rows = rows_dev // 2
    query_units = (
        soft_q.reshape(2, half_rows, local_heads, head_size)
        .transpose(2, 0, 1, 3)
        .reshape(2 * local_heads, half_rows, head_size)
    )

    def head_pieces(source):
        shaped = source.reshape(rows_dev, local_heads, head_size)
        if units == 1:
            shaped = jnp.repeat(shaped, 2, axis=1)
        return shaped.transpose(1, 0, 2)

    query_in, keys_in, values_in = (
        lax.all_to_all(query_units, "seq", split_axis=0, concat_axis=1, tiled=True),
        lax.all_to_all(head_pieces(soft_k), "seq", split_axis=0, concat_axis=1, tiled=True),
        lax.all_to_all(head_pieces(soft_v), "seq", split_axis=0, concat_axis=1, tiled=True),
    )
    seq_len = seq_devices * rows_dev
    query_rows = seq_len // 2
    block_rows = query_rows // 8
    scale = head_size ** (-0.5)
    outputs = []
    for unit_index in range(units):
        half_index = (seq_index * units + unit_index) % 2
        head_slot = unit_index // 2
        pieces = []
        for block_index in range(8):
            key_count = (block_index + 1) * seq_len // 8
            block_q = query_in[
                unit_index, block_index * block_rows : (block_index + 1) * block_rows
            ]
            block_k = keys_in[head_slot, :key_count]
            block_v = values_in[head_slot, :key_count]
            scores = (
                jnp.einsum("qd,kd->qk", block_q, block_k, preferred_element_type=jnp.float32)
                * scale
            )
            local_rows = block_index * block_rows + lax.broadcasted_iota(
                jnp.int32, (block_rows, 1), 0
            )
            positions_q = (
                local_rows // half_rows * rows_dev + half_index * half_rows + local_rows % half_rows
            )
            positions_k = lax.broadcasted_iota(jnp.int32, (1, key_count), 1)
            scores = jnp.where(positions_k <= positions_q, scores, -1e30)
            largest = jnp.max(scores, axis=1, keepdims=True)
            exponent = jnp.exp(scores - largest)
            denominator = jnp.sum(exponent, axis=1, keepdims=True)
            weights = exponent.astype(jnp.bfloat16)
            numerator = jnp.dot(weights, block_v, preferred_element_type=jnp.float32)
            pieces.append((numerator / denominator).astype(jnp.bfloat16))
        outputs.append(jnp.concatenate(pieces, axis=0))
    unit_out = jnp.stack(outputs, axis=0)
    returned = lax.all_to_all(unit_out, "seq", split_axis=1, concat_axis=0, tiled=True)
    soft_out = (
        returned.reshape(local_heads, 2, half_rows, head_size)
        .transpose(1, 2, 0, 3)
        .reshape(rows_dev, width_dev)
    )
    return (lin_out, soft_out)


def line_of_four(lin_q, lin_k, lin_v, lin_gain, soft_q, soft_k, soft_v):
    rows, width = lin_q.shape
    heads = width // HEAD_DIM
    half = heads // 2
    index = lax.axis_index("seq")
    core = index % 2
    place = jnp.stack([index // 2, core]).astype(jnp.int32)
    swap = [(i, i ^ 1) for i in range(8)]
    count = len(CHUNKS)
    offsets = [sum(CHUNKS[:i]) for i in range(count)]
    columns = [slice(o * HEAD_DIM, (o + c) * HEAD_DIM) for o, c in zip(offsets, CHUNKS)]

    key_values = jnp.concatenate([soft_k, soft_v], axis=0)
    first, second, far = [], [], []
    for i in range(count):
        query = soft_q[:, columns[i]]
        first.append(lax.ppermute(query, "seq", [(4, 2), (5, 3), (6, 4), (7, 5)]))
        second.append(lax.ppermute(query, "seq", [(6, 2), (7, 3)]))
        far.append(lax.ppermute(key_values[:, columns[i]], "seq", [(0, 2), (1, 3)]))
    sib_kv = lax.ppermute(key_values, "seq", swap)

    states = own_states(lin_k, lin_v)
    sib_states = lax.ppermute(states, "seq", swap)
    chip_states = lax.dynamic_slice_in_dim(states + sib_states, core * half, half, axis=0)
    before = jnp.zeros((half, HEAD_DIM, HEAD_DIM), BF16)
    for hop in range(3):
        running = (chip_states + before.astype(F32)).astype(BF16)
        arrived = lax.ppermute(running, "seq", [(2 * hop, 2 * hop + 2), (2 * hop + 1, 2 * hop + 3)])
        before = jnp.where(index // 2 == hop + 1, arrived, before)
    other = lax.ppermute(before, "seq", swap)
    before = jnp.where(core == 0, jnp.concatenate([before, other], 0), jnp.concatenate([other, before], 0))

    farx, part1, part2 = [], [], []
    behind = place
    for i in range(count):
        farx.append(lax.ppermute(far[i], "seq", [(2, 3), (3, 2)]))
        out1, out2 = serve(after(place, behind), first[i], second[i], key_values, sib_kv, far[i], farx[i], offsets[i])
        part1.append(lax.ppermute(out1, "seq", [(2, 4), (3, 5), (4, 6), (5, 7)]))
        part2.append(lax.ppermute(out2, "seq", [(2, 6), (3, 7)]))
        behind = out1
        if i == 1:
            mixed, squares = mix(after(place, behind), lin_q, lin_k, lin_v, before, sib_states)
            squares = jnp.sum(squares, axis=1)
            behind = mixed
            squares = squares + lax.ppermute(squares, "grp", [(0, 1), (1, 0), (2, 3), (3, 2)])
        if i == 2:
            squares = after(squares, behind)
            squares = squares + lax.ppermute(squares, "grp", [(0, 2), (2, 0), (1, 3), (3, 1)])
    inverse = lax.rsqrt(squares / (HEADS * HEAD_DIM) + epsilon)
    lin_out = (mixed * inverse[:, None] * lin_gain).astype(BF16)
    soft_out = None
    here = after(place, behind)
    for i in range(count):
        soft_out = finish(here, soft_q, key_values, sib_kv, far[i], farx[i], part1[i], part2[i], soft_out, offsets[i])
    return (lin_out, soft_out)


def shards(*arrays):
    heads = arrays[0].shape[1] // HEAD_DIM
    if lax.axis_size("seq") == 8 and lax.axis_size("grp") == 4 and heads == sum(CHUNKS):
        return line_of_four(*arrays)
    return any_ring(*arrays)


def solution(mesh):
    return jax.shard_map(
        shards,
        mesh=mesh,
        in_specs=(
            P("seq", "grp"),
            P("seq", "grp"),
            P("seq", "grp"),
            P("grp"),
            P("seq", "grp"),
            P("seq", "grp"),
            P("seq", "grp"),
        ),
        out_specs=(P("seq", "grp"), P("seq", "grp")),
        check_vma=False,
    )
```

```python
import functools

import jax
import jax.numpy as jnp
from jax import lax
from jax.experimental import pallas as pl
from jax.experimental.pallas import tpu as pltpu
from jax.sharding import PartitionSpec as P

HEADS = 64
HEAD_DIM = 128
LSE_ROWS = 16
OPEN_ROWS = 8
CHUNKS = (2, 2, 2, 2)
STEP = 4
SERVE_US = 0.001
LAST_US = 0.001
OWN_US = 0.001
VMEM = 8 * 1024 * 1024

highest = lax.Precision.HIGHEST
epsilon = 1e-06
F32 = jnp.float32
BF16 = jnp.bfloat16
LOG2 = HEAD_DIM ** (-0.5) * 1.4426950408889634
NT = (((1,), (1,)), ((), ()))
TN = (((0,), (0,)), ((), ()))


def dot_nt(a, b):
    return lax.dot_general(a, b, NT, preferred_element_type=F32)


def dot_tn(a, b):
    return lax.dot_general(a, b, TN, preferred_element_type=F32)


def dot(a, b):
    return jnp.dot(a, b, preferred_element_type=F32)


def split(a):
    high = a.astype(BF16)
    return high, (a - high.astype(F32)).astype(BF16)


def after(value, *others):
    return lax.optimization_barrier((value, *others))[0]


def causal_mask(rows):
    row_ids = lax.broadcasted_iota(jnp.int32, (rows, rows), 0)
    col_ids = lax.broadcasted_iota(jnp.int32, (rows, rows), 1)
    return col_ids <= row_ids


def lanes(ref, head):
    return ref[:, head * HEAD_DIM : (head + 1) * HEAD_DIM]


def weigh(scores, values, top):
    both = None
    for score, value in zip(scores, values):
        weights = jnp.exp2(score * LOG2 - top).astype(BF16)
        part = dot(weights, jnp.concatenate([value, jnp.ones_like(value)], axis=1))
        both = part if both is None else both + part
    return both[:, :HEAD_DIM], both[:, HEAD_DIM:]


def attend(query, keys, values, mask=None):
    scores = [dot_nt(query, key) for key in keys]
    if mask is not None:
        scores[-1] = jnp.where(mask, scores[-1], -1e30)
    top = jnp.max(functools.reduce(jnp.maximum, scores), axis=1, keepdims=True) * LOG2
    numerator, total = weigh(scores, values, top)
    return numerator * (1.0 / total), top + jnp.log2(total)


def level_rows(level, tile, pieces):
    rows = level.shape[0]
    across = jnp.transpose(level)[:1]
    parts = []
    for _ in range(pieces):
        part = across if pieces == 1 else across.astype(BF16).astype(F32)
        across = across - part
        parts += [part[:, i : i + HEAD_DIM] for i in range(0, rows, HEAD_DIM)]
    parts.append(jnp.zeros((tile - len(parts), HEAD_DIM), F32))
    return jnp.concatenate(parts, axis=0)


def read_level(packed, rows, pieces):
    halves = rows // HEAD_DIM
    level = packed.astype(F32)
    columns = []
    for i in range(halves):
        line = sum(level[j * halves + i : j * halves + i + 1] for j in range(pieces))
        columns.append(jnp.transpose(jnp.broadcast_to(line, (HEAD_DIM, HEAD_DIM))))
    return jnp.concatenate(columns, axis=0)


def blocks_of(ref, head, rows):
    both = lanes(ref, head)
    return [both[i : i + rows] for i in range(0, ref.shape[0], rows)]


def across(head):
    return slice(head * HEAD_DIM, (head + 1) * HEAD_DIM)


def gather(refs, head, rows):
    blocks = [blocks_of(ref, head, rows) for ref in refs]
    return sum((b[:2] for b in blocks), []), sum((b[2:] for b in blocks), [])


def run(copies):
    for copy in copies:
        copy.start()
    for copy in copies:
        copy.wait()


def serve_kernel(together, place, first_hbm, second_hbm, near_hbm, far_hbm, *rest):
    sent_hbm, (first_ref, second_ref, near_ref, far_ref, sent_ref, sems) = rest[:-6], rest[-6:]
    pair, width = first_ref.shape
    rows = pair // 2
    size = pair + 2 * LSE_ROWS
    answers = [sent_hbm[0].at[pl.ds(0, size)], sent_hbm[0].at[pl.ds(size, size)]] if together else sent_hbm

    def copies(pairs):
        return [pltpu.make_async_copy(src, dst, sems.at[i]) for i, (src, dst) in enumerate(pairs)]

    @pl.when(place[0] == 1)
    def _():
        run(copies([(near_hbm, near_ref), (far_hbm, far_ref), (first_hbm, first_ref), (second_hbm, second_ref)]))
        for head in range(width // HEAD_DIM):
            keys, values = gather([near_ref, far_ref], head, rows)
            for slot, query_ref in enumerate([first_ref, second_ref]):
                for i in range(2):
                    part, level = attend(query_ref[i * rows : (i + 1) * rows, across(head)], keys, values)
                    sent_ref[slot, i * rows : (i + 1) * rows, across(head)] = part.astype(BF16)
                    there = slice(pair + i * LSE_ROWS, pair + (i + 1) * LSE_ROWS)
                    sent_ref[slot, there, across(head)] = level_rows(level, LSE_ROWS, 3).astype(BF16)
        run(copies([(sent_ref.at[0], answers[0]), (sent_ref.at[1], answers[1])]))


def own_kernel(place, query_hbm, near_hbm, far_hbm, closed_hbm, open_hbm, query_ref, near_ref, far_ref, closed_ref, open_ref, sems):
    pair, width = query_ref.shape
    rows = pair // 2
    chip = place[0]
    mask = causal_mask(rows)

    def copies(pairs):
        return [pltpu.make_async_copy(src, dst, sems.at[i]) for i, (src, dst) in enumerate(pairs)]

    def attend_own(refs, closed):
        for head in range(width // HEAD_DIM):
            near = blocks_of(near_ref, head, rows)
            keys, values = gather(refs, head, rows)
            for i in range(2):
                here = slice(i * rows, (i + 1) * rows)
                part, level = attend(query_ref[here, across(head)], keys + near[: i + 1], values + near[2 : 3 + i], mask)
                if closed:
                    closed_ref[here, across(head)] = part.astype(BF16)
                else:
                    open_ref[here, across(head)] = part
                    there = slice(pair + i * OPEN_ROWS, pair + (i + 1) * OPEN_ROWS)
                    open_ref[there, across(head)] = level_rows(level, OPEN_ROWS, 1)

    fetch = [(near_hbm, near_ref), (query_hbm, query_ref)]

    @pl.when(chip == 0)
    def _():
        run(copies(fetch))
        attend_own([], True)
        run(copies([(closed_ref, closed_hbm)]))

    @pl.when(chip == 1)
    def _():
        run(copies(fetch + [(far_hbm, far_ref)]))
        attend_own([far_ref], True)
        run(copies([(closed_ref, closed_hbm)]))

    @pl.when(chip == 2)
    def _():
        run(copies(fetch))
        attend_own([], False)
        run(copies([(open_ref, open_hbm)]))

    @pl.when(chip == 3)
    def _():
        run(copies(fetch + [(far_hbm, far_ref)]))
        attend_own([far_ref], False)
        run(copies([(open_ref, open_hbm)]))


def finish_kernel(spans, place, *refs):
    count = len(spans)
    inputs, (keep_hbm, give_hbm, open_ref, part_ref, out_ref, sems) = refs[: 4 * count], refs[4 * count :]
    rows = keep_hbm.shape[0]
    pair, width = 2 * rows, out_ref.shape[2]
    size = pair + 2 * LSE_ROWS
    chip, core = place[0], place[1]

    def hand_out():
        def copies(early_hbm, late_hbm):
            moves = []
            for c in range(count):
                for half, target in enumerate((early_hbm, late_hbm)):
                    there = target.at[:, pl.ds(c * width, width)]
                    moves.append(pltpu.make_async_copy(out_ref.at[c, pl.ds(half * rows, rows)], there, sems.at[2 * c + half]))
            run(moves)

        @pl.when(core == 0)
        def _():
            copies(keep_hbm, give_hbm)

        @pl.when(core == 1)
        def _():
            copies(give_hbm, keep_hbm)

    def merge(which):
        fetch = []
        for c, starts in enumerate(spans):
            moves = [
                pltpu.make_async_copy(inputs[4 * c], open_ref.at[c], sems.at[2 * c]),
                pltpu.make_async_copy(inputs[4 * c + which].at[pl.ds(starts[which - 1], size)], part_ref.at[c], sems.at[2 * c + 1]),
            ]
            for move in moves:
                move.start()
            fetch.append(moves)
        for c in range(count):
            for move in fetch[c]:
                move.wait()
            for head in range(width // HEAD_DIM):
                lane = across(head)
                for i in range(2):
                    here = slice(i * rows, (i + 1) * rows)
                    there = slice(pair + i * OPEN_ROWS, pair + (i + 1) * OPEN_ROWS)
                    terms = [(open_ref[c, here, lane], read_level(open_ref[c, there, lane], rows, 1))]
                    there = slice(pair + i * LSE_ROWS, pair + (i + 1) * LSE_ROWS)
                    terms.append((part_ref[c, here, lane].astype(F32), read_level(part_ref[c, there, lane], rows, 3)))
                    top = functools.reduce(jnp.maximum, [level for _, level in terms])
                    weights = [jnp.exp2(level - top) for _, level in terms]
                    mixed = sum(weight * part for weight, (part, _) in zip(weights, terms))
                    out_ref[c, here, lane] = (mixed * (1.0 / sum(weights))).astype(BF16)
        hand_out()

    @pl.when(chip <= 1)
    def _():
        run([pltpu.make_async_copy(inputs[4 * c + 3], out_ref.at[c], sems.at[c]) for c in range(count)])
        hand_out()

    @pl.when(chip == 2)
    def _():
        merge(1)

    @pl.when(chip == 3)
    def _():
        merge(2)


def col_block(rows, step, offset=0):
    return pl.BlockSpec((rows, step * HEAD_DIM), lambda h: (0, offset // step + h))


SMEM_SPEC = pl.BlockSpec(memory_space=pltpu.SMEM)
ANY_SPEC = pl.BlockSpec(memory_space=pl.ANY)
STATE_SPEC = pl.BlockSpec((STEP // 2 * HEAD_DIM, 2 * HEAD_DIM), lambda h: (h, 0))
VMEM_SPEC = pl.BlockSpec(memory_space=pltpu.VMEM)


def params():
    return pltpu.CompilerParams(vmem_limit_bytes=VMEM)


def cost(microseconds):
    return pl.CostEstimate(flops=int(microseconds * 1.1e9), bytes_accessed=1, transcendentals=0)


def tiny():
    return pl.CostEstimate(flops=1, bytes_accessed=1, transcendentals=0)


def serve(place, first, second, near, far, together, microseconds):
    pair, width = first.shape
    size = pair + 2 * LSE_ROWS
    sent = [(2 * size, width)] if together else [(size, width)] * 2
    return pl.pallas_call(
        functools.partial(serve_kernel, together),
        out_shape=[jax.ShapeDtypeStruct(x, BF16) for x in sent],
        in_specs=[SMEM_SPEC] + [ANY_SPEC] * 4,
        out_specs=[ANY_SPEC] * len(sent),
        scratch_shapes=[pltpu.VMEM(x.shape, BF16) for x in (first, second, near, far)]
        + [pltpu.VMEM((2, size, width), BF16), pltpu.SemaphoreType.DMA((4,))],
        compiler_params=params(),
        cost_estimate=cost(microseconds),
        name="serve",
    )(place, first, second, near, far)


def attend_here(place, query, near, far):
    opened = (query.shape[0] + 2 * OPEN_ROWS, query.shape[1])
    return pl.pallas_call(
        own_kernel,
        out_shape=[jax.ShapeDtypeStruct(query.shape, BF16), jax.ShapeDtypeStruct(opened, F32)],
        in_specs=[SMEM_SPEC] + [ANY_SPEC] * 3,
        out_specs=[ANY_SPEC] * 2,
        scratch_shapes=[pltpu.VMEM(x.shape, BF16) for x in (query, near, far, query)]
        + [pltpu.VMEM(opened, F32), pltpu.SemaphoreType.DMA((3,))],
        compiler_params=params(),
        cost_estimate=cost(OWN_US),
        name="own",
    )(place, query, near, far)


def finish(place, chunks, spans):
    count = len(chunks)
    pair, width = chunks[0][3].shape
    out = jax.ShapeDtypeStruct((pair // 2, count * width), BF16)
    part = (count, pair + 2 * LSE_ROWS, width)
    return pl.pallas_call(
        functools.partial(finish_kernel, spans),
        out_shape=(out, out),
        in_specs=[SMEM_SPEC] + [ANY_SPEC] * (4 * count),
        out_specs=(ANY_SPEC, ANY_SPEC),
        scratch_shapes=[
            pltpu.VMEM((count, *chunks[0][0].shape), F32),
            pltpu.VMEM(part, BF16),
            pltpu.VMEM((count, pair, width), BF16),
            pltpu.SemaphoreType.DMA((2 * count,)),
        ],
        compiler_params=params(),
        cost_estimate=tiny(),
        name="finish",
    )(place, *[x for chunk in chunks for x in chunk])


def state_place(head):
    return slice(head // 2 * HEAD_DIM, (head // 2 + 1) * HEAD_DIM), slice(head % 2 * HEAD_DIM, (head % 2 + 1) * HEAD_DIM)


def state_kernel(key_ref, value_ref, state_ref):
    for head in range(STEP):
        state_ref[state_place(head)] = dot_tn(lanes(key_ref, head), lanes(value_ref, head))


def own_states(keys, values):
    rows, width = keys.shape
    heads = width // HEAD_DIM
    return pl.pallas_call(
        state_kernel,
        grid=(heads // STEP,),
        out_shape=jax.ShapeDtypeStruct((heads // 2 * HEAD_DIM, 2 * HEAD_DIM), F32),
        in_specs=[col_block(rows, STEP), col_block(rows, STEP)],
        out_specs=STATE_SPEC,
        compiler_params=params(),
        cost_estimate=cost(1.0),
        name="states",
    )(keys, values)


def mix_kernel(place, query_ref, key_ref, value_ref, before_ref, sib_ref, mixed_ref, square_ref):
    rows, width = query_ref.shape
    mask = causal_mask(rows)
    squares = jnp.zeros((rows, HEAD_DIM), F32)
    for head in range(width // HEAD_DIM):
        query, value = lanes(query_ref, head), lanes(value_ref, head)
        high, low = split(jnp.where(mask, dot_nt(query, lanes(key_ref, head)), 0.0))
        state = state_place(head)
        prefix = before_ref[state].astype(F32) + jnp.where(place[1] == 1, sib_ref[state], 0.0)
        prefix_high, prefix_low = split(prefix)
        mixed = dot(high, value) + dot(low, value) + dot(query, prefix_high) + dot(query, prefix_low)
        mixed_ref[:, head * HEAD_DIM : (head + 1) * HEAD_DIM] = mixed
        squares = squares + mixed * mixed

    @pl.when(pl.program_id(0) == 0)
    def _():
        square_ref[...] = squares

    @pl.when(pl.program_id(0) > 0)
    def _():
        square_ref[...] += squares

    @pl.when(pl.program_id(0) == pl.num_programs(0) - 1)
    def _():
        square_ref[...] = jnp.broadcast_to(jnp.sum(square_ref[...], axis=1, keepdims=True), square_ref.shape)


def mix(place, queries, keys, values, before, sib_state):
    rows, width = keys.shape
    heads = width // HEAD_DIM
    return pl.pallas_call(
        mix_kernel,
        grid=(heads // STEP,),
        out_shape=(jax.ShapeDtypeStruct((rows, width), F32), jax.ShapeDtypeStruct((rows, HEAD_DIM), F32)),
        in_specs=[SMEM_SPEC, col_block(rows, STEP), col_block(rows, STEP), col_block(rows, STEP), STATE_SPEC, STATE_SPEC],
        out_specs=(col_block(rows, STEP), pl.BlockSpec((rows, HEAD_DIM), lambda h: (0, 0))),
        compiler_params=params(),
        cost_estimate=tiny(),
        name="mix",
    )(place, queries, keys, values, before, sib_state)


def from_behind(value, axis, by):
    peers = lax.axis_size(axis)
    pairs = [(i, i + by) for i in range(peers) if 0 <= i + by < peers]
    return lax.ppermute(value, axis, pairs)


def any_ring(lin_q, lin_k, lin_v, lin_gain, soft_q, soft_k, soft_v):
    rows_dev, width_dev = lin_q.shape
    head_size = HEAD_DIM
    local_heads = width_dev // head_size
    queries_low = lin_q.reshape(rows_dev, local_heads, head_size)
    keys_low = lin_k.reshape(rows_dev, local_heads, head_size)
    values_low = lin_v.reshape(rows_dev, local_heads, head_size)
    queries = queries_low.astype(jnp.float32)
    values_lin = values_low.astype(jnp.float32)
    own_state = jnp.einsum("thd,the->hde", keys_low, values_low, preferred_element_type=jnp.float32)
    zero_state = jnp.zeros_like(own_state)

    def relay_step(counter, running):
        return from_behind(running + own_state, "seq", 1)

    prefix = lax.fori_loop(0, lax.axis_size("seq") - 1, relay_step, zero_state)
    row_ids = lax.broadcasted_iota(jnp.int32, (rows_dev, rows_dev), 0)
    col_ids = lax.broadcasted_iota(jnp.int32, (rows_dev, rows_dev), 1)
    causal = (col_ids <= row_ids).astype(jnp.float32)
    scores_lin = (
        jnp.einsum("thd,shd->hts", queries_low, keys_low, preferred_element_type=jnp.float32)
        * causal[None]
    )
    within = jnp.einsum("hts,she->the", scores_lin, values_lin, precision=highest)
    carried = jnp.einsum("thd,hde->the", queries, prefix, precision=highest)
    mixed_out = (within + carried).reshape(rows_dev, width_dev)
    squares = jnp.sum(mixed_out * mixed_out, axis=1)
    summed = lax.psum(squares, "grp")
    inverse = lax.rsqrt(summed / (HEADS * head_size) + epsilon)
    lin_out = (mixed_out * inverse[:, None] * lin_gain).astype(jnp.bfloat16)
    seq_devices = lax.axis_size("seq")
    seq_index = lax.axis_index("seq")
    units = 2 * local_heads // seq_devices
    half_rows = rows_dev // 2
    query_units = (
        soft_q.reshape(2, half_rows, local_heads, head_size)
        .transpose(2, 0, 1, 3)
        .reshape(2 * local_heads, half_rows, head_size)
    )

    def head_pieces(source):
        shaped = source.reshape(rows_dev, local_heads, head_size)
        if units == 1:
            shaped = jnp.repeat(shaped, 2, axis=1)
        return shaped.transpose(1, 0, 2)

    query_in, keys_in, values_in = (
        lax.all_to_all(query_units, "seq", split_axis=0, concat_axis=1, tiled=True),
        lax.all_to_all(head_pieces(soft_k), "seq", split_axis=0, concat_axis=1, tiled=True),
        lax.all_to_all(head_pieces(soft_v), "seq", split_axis=0, concat_axis=1, tiled=True),
    )
    seq_len = seq_devices * rows_dev
    query_rows = seq_len // 2
    block_rows = query_rows // 8
    scale = head_size ** (-0.5)
    outputs = []
    for unit_index in range(units):
        half_index = (seq_index * units + unit_index) % 2
        head_slot = unit_index // 2
        pieces = []
        for block_index in range(8):
            key_count = (block_index + 1) * seq_len // 8
            block_q = query_in[
                unit_index, block_index * block_rows : (block_index + 1) * block_rows
            ]
            block_k = keys_in[head_slot, :key_count]
            block_v = values_in[head_slot, :key_count]
            scores = (
                jnp.einsum("qd,kd->qk", block_q, block_k, preferred_element_type=jnp.float32)
                * scale
            )
            local_rows = block_index * block_rows + lax.broadcasted_iota(
                jnp.int32, (block_rows, 1), 0
            )
            positions_q = (
                local_rows // half_rows * rows_dev + half_index * half_rows + local_rows % half_rows
            )
            positions_k = lax.broadcasted_iota(jnp.int32, (1, key_count), 1)
            scores = jnp.where(positions_k <= positions_q, scores, -1e30)
            largest = jnp.max(scores, axis=1, keepdims=True)
            exponent = jnp.exp(scores - largest)
            denominator = jnp.sum(exponent, axis=1, keepdims=True)
            weights = exponent.astype(jnp.bfloat16)
            numerator = jnp.dot(weights, block_v, preferred_element_type=jnp.float32)
            pieces.append((numerator / denominator).astype(jnp.bfloat16))
        outputs.append(jnp.concatenate(pieces, axis=0))
    unit_out = jnp.stack(outputs, axis=0)
    returned = lax.all_to_all(unit_out, "seq", split_axis=1, concat_axis=0, tiled=True)
    soft_out = (
        returned.reshape(local_heads, 2, half_rows, head_size)
        .transpose(1, 2, 0, 3)
        .reshape(rows_dev, width_dev)
    )
    return (lin_out, soft_out)


def line_of_four(lin_q, lin_k, lin_v, lin_gain, soft_q, soft_k, soft_v):
    rows, width = lin_q.shape
    half = width // 2
    index = lax.axis_index("seq")
    core = index % 2
    place = jnp.stack([index // 2, core]).astype(jnp.int32)
    swap = [(i, i ^ 1) for i in range(8)]
    up = [(i, i + 1) for i in range(0, 8, 2)]
    down = [(i + 1, i) for i in range(0, 8, 2)]
    count = len(CHUNKS)
    offsets = [sum(CHUNKS[:i]) for i in range(count)]
    columns = [slice(o * HEAD_DIM, (o + c) * HEAD_DIM) for o, c in zip(offsets, CHUNKS)]

    chip = place[0]

    chip = place[0]

    def prologue():
        here = columns[0]
        there = slice(here.start + half, here.stop + half)
        keep = [jnp.where(core == 0, x[:, here], x[:, there]) for x in (soft_k, soft_v, soft_q)]
        give = jnp.concatenate([jnp.where(core == 0, x[:, there], x[:, here]) for x in (soft_k, soft_v, soft_q)], axis=0)
        got = lax.ppermute(give, "seq", swap)
        both = [(x, got[i * rows : (i + 1) * rows]) for i, x in enumerate(keep)]
        ordered = [jnp.where(core == 0, jnp.concatenate([x, y]), jnp.concatenate([y, x])) for x, y in both]
        return jnp.concatenate(ordered[:2], axis=0), ordered[2]

    def chunk(sources, i):
        here, there = columns[i], slice(columns[i].start + half, columns[i].stop + half)
        low = [x[:, here] for pair in sources for x in pair]
        high = [x[:, there] for pair in sources for x in pair[::-1]]
        return jnp.concatenate([jnp.where(core == 0, x, y) for x, y in zip(low, high)], axis=0)

    first, second, far, query, near = [], [], [], [], []

    def send(i, *behind):
        far.append(lax.ppermute(after(near[i], *behind), "seq", [(0, 2), (1, 3), (4, 6), (5, 7)]))
        source = after(query[i], *behind)
        first.append(lax.ppermute(source, "seq", [(4, 2), (5, 3)]))
        second.append(lax.ppermute(source, "seq", [(6, 2), (7, 3)]))

    near_0, query_0 = prologue()
    near.append(near_0)
    query.append(query_0)
    send(0)
    keys, values, queries = [(x, lax.ppermute(after(x, near_0), "seq", swap)) for x in (soft_k, soft_v, soft_q)]
    states = own_states(after(lin_k, query_0), lin_v)
    sib_states = lax.ppermute(states, "seq", swap)
    for i in range(1, count):
        near.append(chunk([keys, values], i))
        query.append(chunk([queries], i))
    state_rows = states.shape[0] // 2
    chip_states = lax.dynamic_slice_in_dim(states + sib_states, core * state_rows, state_rows, axis=0)
    handed = []

    def hop(*behind):
        i = len(handed)
        running = chip_states + handed[-1].astype(F32) if handed else chip_states
        handed.append(lax.ppermute(after(running.astype(BF16), *behind), "seq", [(2 * i, 2 * i + 2), (2 * i + 1, 2 * i + 3)]))

    hop()
    size = 2 * rows + 2 * LSE_ROWS
    part1, part2, served, own = [], [], [], []
    waits = [handed[-1], *near, *query]
    for i in range(count):
        if i >= 2:
            waits.append(part1[i - 2])
        gate = after(place, first[i], second[i], far[i], *waits)
        waits = []
        if i + 1 < count:
            send(i + 1, gate)
        if i == 0 or i == count - 1:
            hop(gate)
            waits.append(handed[-1])
        final = i == count - 1
        if final:
            passed = jnp.concatenate([x[size:] for x in part1[:i - 1]], axis=0)
            passed = lax.ppermute(after(passed, gate), "seq", [(4, 6), (5, 7)])
        served.append(serve(gate, first[i], second[i], near[i], far[i], not final, LAST_US if final else SERVE_US))
        part1.append(lax.ppermute(served[-1][0], "seq", [(2, 4), (3, 5)]))
        if final:
            part2 = lax.ppermute(served[-1][1], "seq", [(2, 6), (3, 7)])
        else:
            own.append(attend_here(after(place, served[-1][0]), query[i], near[i], far[i]))
            waits.append(own[-1][0])
    late = lax.ppermute(after(part1[count - 2], served[-1][0])[size:], "seq", [(4, 6), (5, 7)])
    gate = after(place, served[-1][0], *waits)
    own.append(attend_here(gate, query[-1], near[-1], far[-1]))
    before = jnp.where(chip == 1, handed[0], jnp.where(chip == 2, handed[1], jnp.where(chip == 3, handed[2], 0)))
    other = lax.ppermute(after(before, gate), "seq", swap)
    before = jnp.where(core == 0, jnp.concatenate([before, other]), jnp.concatenate([other, before]))
    mixed, squares = mix(after(gate, own[-1][0]), lin_q, lin_k, lin_v, before, sib_states)

    def complete(which, *behind):
        chunks, spans = [], []
        for i in which:
            other = part2 if i == count - 1 else late if i == count - 2 else passed
            spans.append((0, i * size if i < count - 2 else 0))
            chunks.append((own[i][1], part1[i], other, own[i][0]))
        return finish(after(place, *behind), chunks, tuple(spans))

    keep, give = complete(range(count - 1), mixed)
    got = lax.ppermute(give, "seq", swap)
    squares = squares + lax.ppermute(squares, "grp", [(0, 1), (1, 0), (2, 3), (3, 2)])
    squares = after(squares, keep)
    squares = squares + lax.ppermute(squares, "grp", [(0, 2), (2, 0), (1, 3), (3, 1)])
    keep_last, give_last = complete([count - 1], keep)
    got_last = lax.ppermute(give_last, "seq", swap)
    inverse = lax.rsqrt(after(squares, keep_last)[:, :1] / (HEADS * HEAD_DIM) + epsilon)
    lin_out = (mixed * inverse * lin_gain).astype(BF16)
    here, there = [keep, keep_last], [got, got_last]
    soft_out = jnp.where(core == 0, jnp.concatenate(here + there, axis=1), jnp.concatenate(there + here, axis=1))
    return (lin_out, soft_out)


def shards(*arrays):
    heads = arrays[0].shape[1] // HEAD_DIM
    if lax.axis_size("seq") == 8 and lax.axis_size("grp") == 4 and heads == 2 * sum(CHUNKS):
        return line_of_four(*arrays)
    return any_ring(*arrays)


def solution(mesh):
    return jax.shard_map(
        shards,
        mesh=mesh,
        in_specs=(
            P("seq", "grp"),
            P("seq", "grp"),
            P("seq", "grp"),
            P("grp"),
            P("seq", "grp"),
            P("seq", "grp"),
            P("seq", "grp"),
        ),
        out_specs=(P("seq", "grp"), P("seq", "grp")),
        check_vma=False,
    )
```

```python
import functools

import jax
import jax.numpy as jnp
from jax import lax
from jax.experimental import pallas as pl
from jax.experimental.pallas import tpu as pltpu
from jax.sharding import PartitionSpec as P

HEADS = 64
HEAD_DIM = 128
LSE_ROWS = 16
OPEN_ROWS = 8
PAD_ROWS = 16
CHUNKS = (2, 2, 2, 2)
STEP = 4
SERVE_US = 0.001
LAST_US = 0.001
FINISH_US = 30.0
OWN_US = 0.001
VMEM = 8 * 1024 * 1024

highest = lax.Precision.HIGHEST
epsilon = 1e-06
F32 = jnp.float32
BF16 = jnp.bfloat16
LOG2 = HEAD_DIM ** (-0.5) * 1.4426950408889634
NT = (((1,), (1,)), ((), ()))
TN = (((0,), (0,)), ((), ()))


def dot_nt(a, b):
    return lax.dot_general(a, b, NT, preferred_element_type=F32)


def dot_tn(a, b):
    return lax.dot_general(a, b, TN, preferred_element_type=F32)


def dot(a, b):
    return jnp.dot(a, b, preferred_element_type=F32)


def split(a):
    high = a.astype(BF16)
    return high, (a - high.astype(F32)).astype(BF16)


def after(value, *others):
    return lax.optimization_barrier((value, *others))[0]


def causal_mask(rows):
    row_ids = lax.broadcasted_iota(jnp.int32, (rows, rows), 0)
    col_ids = lax.broadcasted_iota(jnp.int32, (rows, rows), 1)
    return col_ids <= row_ids


def lanes(ref, head):
    return ref[:, head * HEAD_DIM : (head + 1) * HEAD_DIM]


def weigh(scores, values, top):
    both = None
    for score, value in zip(scores, values):
        weights = jnp.exp2(score * LOG2 - top).astype(BF16)
        part = dot(weights, jnp.concatenate([value, jnp.ones_like(value)], axis=1))
        both = part if both is None else both + part
    return both[:, :HEAD_DIM], both[:, HEAD_DIM:]


def attend(query, keys, values, mask=None):
    scores = [dot_nt(query, key) for key in keys]
    if mask is not None:
        scores[-1] = jnp.where(mask, scores[-1], -1e30)
    top = jnp.max(functools.reduce(jnp.maximum, scores), axis=1, keepdims=True) * LOG2
    numerator, total = weigh(scores, values, top)
    return numerator * (1.0 / total), top + jnp.log2(total)


def level_rows(level, tile, pieces):
    rows = level.shape[0]
    across = jnp.transpose(level)[:1]
    parts = []
    for _ in range(pieces):
        part = across if pieces == 1 else across.astype(BF16).astype(F32)
        across = across - part
        parts += [part[:, i : i + HEAD_DIM] for i in range(0, rows, HEAD_DIM)]
    parts.append(jnp.zeros((tile - len(parts), HEAD_DIM), F32))
    return jnp.concatenate(parts, axis=0)


def read_level(packed, rows, pieces):
    halves = rows // HEAD_DIM
    level = packed.astype(F32)
    columns = []
    for i in range(halves):
        line = sum(level[j * halves + i : j * halves + i + 1] for j in range(pieces))
        columns.append(jnp.transpose(jnp.broadcast_to(line, (HEAD_DIM, HEAD_DIM))))
    return jnp.concatenate(columns, axis=0)


def blocks_of(ref, head, rows):
    both = lanes(ref, head)
    return [both[i : i + rows] for i in range(0, ref.shape[0], rows)]


def across(head):
    return slice(head * HEAD_DIM, (head + 1) * HEAD_DIM)


def gather(refs, head, rows):
    blocks = [blocks_of(ref, head, rows) for ref in refs]
    return sum((b[:2] for b in blocks), []), sum((b[2:] for b in blocks), [])


def run(copies):
    for copy in copies:
        copy.start()
    for copy in copies:
        copy.wait()


def serve_kernel(together, place, first_hbm, second_hbm, near_hbm, far_hbm, *rest):
    sent_hbm, (first_ref, second_ref, near_ref, far_ref, sent_ref, sems) = rest[:-6], rest[-6:]
    pair, width = near_ref.shape[0] // 2, near_ref.shape[1]
    rows = pair // 2
    size = pair + 2 * LSE_ROWS
    answers = [sent_hbm[0].at[pl.ds(0, size)], sent_hbm[0].at[pl.ds(size, size)]] if together else sent_hbm

    def copies(pairs):
        return [pltpu.make_async_copy(src, dst, sems.at[i]) for i, (src, dst) in enumerate(pairs)]

    @pl.when(place[0] == 1)
    def _():
        run(copies([(near_hbm, near_ref), (far_hbm, far_ref), (first_hbm, first_ref), (second_hbm, second_ref)]))
        if not together:
            sent_ref[:, size:] = jnp.zeros_like(sent_ref[:, size:])
        for head in range(width // HEAD_DIM):
            keys, values = gather([near_ref, far_ref], head, rows)
            for slot, query_ref in enumerate([first_ref, second_ref]):
                for i in range(2):
                    part, level = attend(query_ref[i * rows : (i + 1) * rows, across(head)], keys, values)
                    sent_ref[slot, i * rows : (i + 1) * rows, across(head)] = part.astype(BF16)
                    there = slice(pair + i * LSE_ROWS, pair + (i + 1) * LSE_ROWS)
                    sent_ref[slot, there, across(head)] = level_rows(level, LSE_ROWS, 3).astype(BF16)
        run(copies([(sent_ref.at[0], answers[0]), (sent_ref.at[1], answers[1])]))


def own_kernel(place, query_hbm, near_hbm, far_hbm, closed_hbm, open_hbm, query_ref, near_ref, far_ref, closed_ref, open_ref, sems):
    pair, width = near_ref.shape[0] // 2, near_ref.shape[1]
    rows = pair // 2
    chip = place[0]
    mask = causal_mask(rows)

    def copies(pairs):
        return [pltpu.make_async_copy(src, dst, sems.at[i]) for i, (src, dst) in enumerate(pairs)]

    def attend_own(refs, closed):
        for head in range(width // HEAD_DIM):
            near = blocks_of(near_ref, head, rows)
            keys, values = gather(refs, head, rows)
            for i in range(2):
                here = slice(i * rows, (i + 1) * rows)
                part, level = attend(query_ref[here, across(head)], keys + near[: i + 1], values + near[2 : 3 + i], mask)
                if closed:
                    closed_ref[here, across(head)] = part.astype(BF16)
                else:
                    open_ref[here, across(head)] = part
                    there = slice(pair + i * OPEN_ROWS, pair + (i + 1) * OPEN_ROWS)
                    open_ref[there, across(head)] = level_rows(level, OPEN_ROWS, 1)

    fetch = [(near_hbm, near_ref), (query_hbm, query_ref)]

    @pl.when(chip == 0)
    def _():
        run(copies(fetch))
        attend_own([], True)
        run(copies([(closed_ref, closed_hbm)]))

    @pl.when(chip == 1)
    def _():
        run(copies(fetch + [(far_hbm, far_ref)]))
        attend_own([far_ref], True)
        run(copies([(closed_ref, closed_hbm)]))

    @pl.when(chip == 2)
    def _():
        run(copies(fetch))
        attend_own([], False)
        run(copies([(open_ref, open_hbm)]))

    @pl.when(chip == 3)
    def _():
        run(copies(fetch + [(far_hbm, far_ref)]))
        attend_own([far_ref], False)
        run(copies([(open_ref, open_hbm)]))


def finish_kernel(spans, place, *refs):
    count = len(spans)
    inputs, (keep_hbm, give_hbm, open_ref, part_ref, out_ref, sems) = refs[: 4 * count], refs[4 * count :]
    rows = keep_hbm.shape[0]
    pair, width = 2 * rows, out_ref.shape[2]
    size = pair + 2 * LSE_ROWS
    chip, core = place[0], place[1]

    def hand_out():
        def copies(early_hbm, late_hbm):
            moves = []
            for c in range(count):
                for half, target in enumerate((early_hbm, late_hbm)):
                    there = target.at[:, pl.ds(c * width, width)]
                    moves.append(pltpu.make_async_copy(out_ref.at[c, pl.ds(half * rows, rows)], there, sems.at[2 * c + half]))
            run(moves)

        @pl.when(core == 0)
        def _():
            copies(keep_hbm, give_hbm)

        @pl.when(core == 1)
        def _():
            copies(give_hbm, keep_hbm)

    def merge(which):
        fetch = []
        for c, starts in enumerate(spans):
            moves = [
                pltpu.make_async_copy(inputs[4 * c], open_ref.at[c], sems.at[2 * c]),
                pltpu.make_async_copy(inputs[4 * c + which].at[pl.ds(starts[which - 1], size)], part_ref.at[c], sems.at[2 * c + 1]),
            ]
            for move in moves:
                move.start()
            fetch.append(moves)
        for c in range(count):
            for move in fetch[c]:
                move.wait()
            for head in range(width // HEAD_DIM):
                lane = across(head)
                for i in range(2):
                    here = slice(i * rows, (i + 1) * rows)
                    there = slice(pair + i * OPEN_ROWS, pair + (i + 1) * OPEN_ROWS)
                    terms = [(open_ref[c, here, lane], read_level(open_ref[c, there, lane], rows, 1))]
                    there = slice(pair + i * LSE_ROWS, pair + (i + 1) * LSE_ROWS)
                    terms.append((part_ref[c, here, lane].astype(F32), read_level(part_ref[c, there, lane], rows, 3)))
                    top = functools.reduce(jnp.maximum, [level for _, level in terms])
                    weights = [jnp.exp2(level - top) for _, level in terms]
                    mixed = sum(weight * part for weight, (part, _) in zip(weights, terms))
                    out_ref[c, here, lane] = (mixed * (1.0 / sum(weights))).astype(BF16)
        hand_out()

    @pl.when(chip <= 1)
    def _():
        run([pltpu.make_async_copy(inputs[4 * c + 3], out_ref.at[c], sems.at[c]) for c in range(count)])
        hand_out()

    @pl.when(chip == 2)
    def _():
        merge(1)

    @pl.when(chip == 3)
    def _():
        merge(2)


def col_block(rows, step, offset=0):
    return pl.BlockSpec((rows, step * HEAD_DIM), lambda h: (0, offset // step + h))


SMEM_SPEC = pl.BlockSpec(memory_space=pltpu.SMEM)
ANY_SPEC = pl.BlockSpec(memory_space=pl.ANY)
HBM_SPEC = pl.BlockSpec(memory_space=pltpu.HBM)
STATE_SPEC = pl.BlockSpec((STEP // 2 * HEAD_DIM, 2 * HEAD_DIM), lambda h: (h, 0))
VMEM_SPEC = pl.BlockSpec(memory_space=pltpu.VMEM)


def params():
    return pltpu.CompilerParams(vmem_limit_bytes=VMEM)


def cost(microseconds):
    return pl.CostEstimate(flops=int(microseconds * 1.1e9), bytes_accessed=1, transcendentals=0)


def tiny():
    return pl.CostEstimate(flops=1, bytes_accessed=1, transcendentals=0)


def serve(place, first, second, near, far, together, microseconds):
    pair, width = near.shape[0] // 2, near.shape[1]
    size = pair + 2 * LSE_ROWS + (0 if together else PAD_ROWS)
    sent = [(2 * size, width)] if together else [(size, width)] * 2
    return pl.pallas_call(
        functools.partial(serve_kernel, together),
        out_shape=[jax.ShapeDtypeStruct(x, BF16) for x in sent],
        in_specs=[SMEM_SPEC] + [ANY_SPEC] * 4,
        out_specs=[ANY_SPEC] * len(sent),
        scratch_shapes=[pltpu.VMEM(x.shape, BF16) for x in (first, second, near, far)]
        + [pltpu.VMEM((2, size, width), BF16), pltpu.SemaphoreType.DMA((4,))],
        compiler_params=params(),
        cost_estimate=cost(microseconds),
        name="serve",
    )(place, first, second, near, far)


def attend_here(place, query, near, far):
    closed = (near.shape[0] // 2, near.shape[1])
    opened = (closed[0] + 2 * OPEN_ROWS, closed[1])
    return pl.pallas_call(
        own_kernel,
        out_shape=[jax.ShapeDtypeStruct(closed, BF16), jax.ShapeDtypeStruct(opened, F32)],
        in_specs=[SMEM_SPEC] + [ANY_SPEC] * 3,
        out_specs=[HBM_SPEC] * 2,
        scratch_shapes=[pltpu.VMEM(x, BF16) for x in (query.shape, near.shape, far.shape, closed)]
        + [pltpu.VMEM(opened, F32), pltpu.SemaphoreType.DMA((3,))],
        compiler_params=params(),
        cost_estimate=cost(OWN_US),
        name="own",
    )(place, query, near, far)


def finish(place, chunks, spans, microseconds):
    count = len(chunks)
    pair, width = chunks[0][3].shape
    out = jax.ShapeDtypeStruct((pair // 2, count * width), BF16)
    part = (count, pair + 2 * LSE_ROWS, width)
    return pl.pallas_call(
        functools.partial(finish_kernel, spans),
        out_shape=(out, out),
        in_specs=[SMEM_SPEC] + [HBM_SPEC] * (4 * count),
        out_specs=(ANY_SPEC, ANY_SPEC),
        scratch_shapes=[
            pltpu.VMEM((count, *chunks[0][0].shape), F32),
            pltpu.VMEM(part, BF16),
            pltpu.VMEM((count, pair, width), BF16),
            pltpu.SemaphoreType.DMA((2 * count,)),
        ],
        compiler_params=params(),
        cost_estimate=cost(microseconds),
        name="finish",
    )(place, *[x for chunk in chunks for x in chunk])


def state_place(head):
    return slice(head // 2 * HEAD_DIM, (head // 2 + 1) * HEAD_DIM), slice(head % 2 * HEAD_DIM, (head % 2 + 1) * HEAD_DIM)


def state_kernel(key_ref, value_ref, state_ref):
    for head in range(STEP):
        state_ref[state_place(head)] = dot_tn(lanes(key_ref, head), lanes(value_ref, head))


def own_states(keys, values):
    rows, width = keys.shape
    heads = width // HEAD_DIM
    return pl.pallas_call(
        state_kernel,
        grid=(heads // STEP,),
        out_shape=jax.ShapeDtypeStruct((heads // 2 * HEAD_DIM, 2 * HEAD_DIM), F32),
        in_specs=[col_block(rows, STEP), col_block(rows, STEP)],
        out_specs=STATE_SPEC,
        compiler_params=params(),
        cost_estimate=cost(1.0),
        name="states",
    )(keys, values)


def mix_kernel(place, query_ref, key_ref, value_ref, before_ref, sib_ref, mixed_ref, square_ref):
    rows, width = query_ref.shape
    mask = causal_mask(rows)
    squares = jnp.zeros((rows, HEAD_DIM), F32)
    for head in range(width // HEAD_DIM):
        query, value = lanes(query_ref, head), lanes(value_ref, head)
        high, low = split(jnp.where(mask, dot_nt(query, lanes(key_ref, head)), 0.0))
        state = state_place(head)
        prefix = before_ref[state].astype(F32) + jnp.where(place[1] == 1, sib_ref[state], 0.0)
        prefix_high, prefix_low = split(prefix)
        mixed = dot(high, value) + dot(low, value) + dot(query, prefix_high) + dot(query, prefix_low)
        mixed_ref[:, head * HEAD_DIM : (head + 1) * HEAD_DIM] = mixed
        squares = squares + mixed * mixed

    @pl.when(pl.program_id(0) == 0)
    def _():
        square_ref[...] = squares

    @pl.when(pl.program_id(0) > 0)
    def _():
        square_ref[...] += squares

    @pl.when(pl.program_id(0) == pl.num_programs(0) - 1)
    def _():
        square_ref[...] = jnp.broadcast_to(jnp.sum(square_ref[...], axis=1, keepdims=True), square_ref.shape)


def mix(place, queries, keys, values, before, sib_state):
    rows, width = keys.shape
    heads = width // HEAD_DIM
    return pl.pallas_call(
        mix_kernel,
        grid=(heads // STEP,),
        out_shape=(jax.ShapeDtypeStruct((rows, width), F32), jax.ShapeDtypeStruct((rows, HEAD_DIM), F32)),
        in_specs=[SMEM_SPEC, col_block(rows, STEP), col_block(rows, STEP), col_block(rows, STEP), STATE_SPEC, STATE_SPEC],
        out_specs=(col_block(rows, STEP), pl.BlockSpec((rows, HEAD_DIM), lambda h: (0, 0))),
        compiler_params=params(),
        cost_estimate=tiny(),
        name="mix",
    )(place, queries, keys, values, before, sib_state)


def from_behind(value, axis, by):
    peers = lax.axis_size(axis)
    pairs = [(i, i + by) for i in range(peers) if 0 <= i + by < peers]
    return lax.ppermute(value, axis, pairs)


def any_ring(lin_q, lin_k, lin_v, lin_gain, soft_q, soft_k, soft_v):
    rows_dev, width_dev = lin_q.shape
    head_size = HEAD_DIM
    local_heads = width_dev // head_size
    queries_low = lin_q.reshape(rows_dev, local_heads, head_size)
    keys_low = lin_k.reshape(rows_dev, local_heads, head_size)
    values_low = lin_v.reshape(rows_dev, local_heads, head_size)
    queries = queries_low.astype(jnp.float32)
    values_lin = values_low.astype(jnp.float32)
    own_state = jnp.einsum("thd,the->hde", keys_low, values_low, preferred_element_type=jnp.float32)
    zero_state = jnp.zeros_like(own_state)

    def relay_step(counter, running):
        return from_behind(running + own_state, "seq", 1)

    prefix = lax.fori_loop(0, lax.axis_size("seq") - 1, relay_step, zero_state)
    row_ids = lax.broadcasted_iota(jnp.int32, (rows_dev, rows_dev), 0)
    col_ids = lax.broadcasted_iota(jnp.int32, (rows_dev, rows_dev), 1)
    causal = (col_ids <= row_ids).astype(jnp.float32)
    scores_lin = (
        jnp.einsum("thd,shd->hts", queries_low, keys_low, preferred_element_type=jnp.float32)
        * causal[None]
    )
    within = jnp.einsum("hts,she->the", scores_lin, values_lin, precision=highest)
    carried = jnp.einsum("thd,hde->the", queries, prefix, precision=highest)
    mixed_out = (within + carried).reshape(rows_dev, width_dev)
    squares = jnp.sum(mixed_out * mixed_out, axis=1)
    summed = lax.psum(squares, "grp")
    inverse = lax.rsqrt(summed / (HEADS * head_size) + epsilon)
    lin_out = (mixed_out * inverse[:, None] * lin_gain).astype(jnp.bfloat16)
    seq_devices = lax.axis_size("seq")
    seq_index = lax.axis_index("seq")
    units = 2 * local_heads // seq_devices
    half_rows = rows_dev // 2
    query_units = (
        soft_q.reshape(2, half_rows, local_heads, head_size)
        .transpose(2, 0, 1, 3)
        .reshape(2 * local_heads, half_rows, head_size)
    )

    def head_pieces(source):
        shaped = source.reshape(rows_dev, local_heads, head_size)
        if units == 1:
            shaped = jnp.repeat(shaped, 2, axis=1)
        return shaped.transpose(1, 0, 2)

    query_in, keys_in, values_in = (
        lax.all_to_all(query_units, "seq", split_axis=0, concat_axis=1, tiled=True),
        lax.all_to_all(head_pieces(soft_k), "seq", split_axis=0, concat_axis=1, tiled=True),
        lax.all_to_all(head_pieces(soft_v), "seq", split_axis=0, concat_axis=1, tiled=True),
    )
    seq_len = seq_devices * rows_dev
    query_rows = seq_len // 2
    block_rows = query_rows // 8
    scale = head_size ** (-0.5)
    outputs = []
    for unit_index in range(units):
        half_index = (seq_index * units + unit_index) % 2
        head_slot = unit_index // 2
        pieces = []
        for block_index in range(8):
            key_count = (block_index + 1) * seq_len // 8
            block_q = query_in[
                unit_index, block_index * block_rows : (block_index + 1) * block_rows
            ]
            block_k = keys_in[head_slot, :key_count]
            block_v = values_in[head_slot, :key_count]
            scores = (
                jnp.einsum("qd,kd->qk", block_q, block_k, preferred_element_type=jnp.float32)
                * scale
            )
            local_rows = block_index * block_rows + lax.broadcasted_iota(
                jnp.int32, (block_rows, 1), 0
            )
            positions_q = (
                local_rows // half_rows * rows_dev + half_index * half_rows + local_rows % half_rows
            )
            positions_k = lax.broadcasted_iota(jnp.int32, (1, key_count), 1)
            scores = jnp.where(positions_k <= positions_q, scores, -1e30)
            largest = jnp.max(scores, axis=1, keepdims=True)
            exponent = jnp.exp(scores - largest)
            denominator = jnp.sum(exponent, axis=1, keepdims=True)
            weights = exponent.astype(jnp.bfloat16)
            numerator = jnp.dot(weights, block_v, preferred_element_type=jnp.float32)
            pieces.append((numerator / denominator).astype(jnp.bfloat16))
        outputs.append(jnp.concatenate(pieces, axis=0))
    unit_out = jnp.stack(outputs, axis=0)
    returned = lax.all_to_all(unit_out, "seq", split_axis=1, concat_axis=0, tiled=True)
    soft_out = (
        returned.reshape(local_heads, 2, half_rows, head_size)
        .transpose(1, 2, 0, 3)
        .reshape(rows_dev, width_dev)
    )
    return (lin_out, soft_out)


def line_of_four(lin_q, lin_k, lin_v, lin_gain, soft_q, soft_k, soft_v):
    rows, width = lin_q.shape
    half = width // 2
    index = lax.axis_index("seq")
    core = index % 2
    place = jnp.stack([index // 2, core]).astype(jnp.int32)
    swap = [(i, i ^ 1) for i in range(8)]
    up = [(i, i + 1) for i in range(0, 8, 2)]
    down = [(i + 1, i) for i in range(0, 8, 2)]
    count = len(CHUNKS)
    offsets = [sum(CHUNKS[:i]) for i in range(count)]
    columns = [slice(o * HEAD_DIM, (o + c) * HEAD_DIM) for o, c in zip(offsets, CHUNKS)]

    chip = place[0]

    chip = place[0]

    def prologue():
        here = columns[0]
        there = slice(here.start + half, here.stop + half)
        keep = [jnp.where(core == 0, x[:, here], x[:, there]) for x in (soft_k, soft_v, soft_q)]
        give = jnp.concatenate([jnp.where(core == 0, x[:, there], x[:, here]) for x in (soft_k, soft_v, soft_q)], axis=0)
        got = lax.ppermute(give, "seq", swap)
        both = [(x, got[i * rows : (i + 1) * rows]) for i, x in enumerate(keep)]
        ordered = [jnp.where(core == 0, jnp.concatenate([x, y]), jnp.concatenate([y, x])) for x, y in both]
        return jnp.concatenate(ordered[:2], axis=0), ordered[2]

    def chunk(sources, i):
        here, there = columns[i], slice(columns[i].start + half, columns[i].stop + half)
        low = [x[:, here] for pair in sources for x in pair]
        high = [x[:, there] for pair in sources for x in pair[::-1]]
        return jnp.concatenate([jnp.where(core == 0, x, y) for x, y in zip(low, high)], axis=0)

    first, second, far, query, near = [], [], [], [], []

    def send(i, *behind):
        far.append(lax.ppermute(after(near[i], *behind), "seq", [(0, 2), (1, 3), (4, 6), (5, 7)]))
        source = after(query[i], *behind)
        first.append(lax.ppermute(source, "seq", [(4, 2), (5, 3)]))
        second.append(lax.ppermute(source, "seq", [(6, 2), (7, 3)]))

    near_0, query_0 = prologue()
    near.append(near_0)
    query.append(jnp.pad(query_0, ((0, PAD_ROWS), (0, 0))))
    send(0)
    keys, values, queries = [(x, lax.ppermute(after(x, near_0), "seq", swap)) for x in (soft_k, soft_v, soft_q)]
    states = own_states(after(lin_k, query_0), lin_v)
    sib_states = lax.ppermute(states, "seq", swap)
    for i in range(1, count):
        near.append(chunk([keys, values], i))
        query.append(jnp.pad(chunk([queries], i), ((0, PAD_ROWS), (0, 0))))
    state_rows = states.shape[0] // 2
    chip_states = lax.dynamic_slice_in_dim(states + sib_states, core * state_rows, state_rows, axis=0)
    handed = []

    def hop(*behind):
        i = len(handed)
        running = chip_states + handed[-1].astype(F32) if handed else chip_states
        running = after(running.astype(BF16), *behind)
        if i == 2:
            running = jnp.pad(running, ((0, state_rows // 2), (0, 0)))
        sent = lax.ppermute(running, "seq", [(2 * i, 2 * i + 2), (2 * i + 1, 2 * i + 3)])
        handed.append(sent[:state_rows])

    hop()
    size = 2 * rows + 2 * LSE_ROWS
    part1, part2, served, own = [], [], [], []
    waits = [*near, *query]
    for i in range(count):
        if i >= 2:
            waits.append(part1[i - 2])
        gate = after(place, first[i], second[i], far[i])
        gate = after(gate, *waits)
        waits = []
        if i + 1 < count:
            send(i + 1, gate)
        if i == count - 1:
            hop(gate)
            waits.append(handed[-1])
        final = i == count - 1
        if final:
            passed = jnp.concatenate([x[size:] for x in part1[:i - 1]], axis=0)
            passed = lax.ppermute(after(passed, gate), "seq", [(4, 6), (5, 7)])
        served.append(serve(gate, first[i], second[i], near[i], far[i], not final, LAST_US if final else SERVE_US))
        part1.append(lax.ppermute(served[-1][0], "seq", [(2, 4), (3, 5)]))
        if final:
            part2 = lax.ppermute(served[-1][1], "seq", [(2, 6), (3, 7)])
        else:
            own.append(attend_here(after(place, served[-1][0]), query[i], near[i], far[i]))
            waits.append(own[-1][0])
            if i == 0:
                hop(own[-1][0])
                waits.append(handed[-1])
    gate = after(place, served[-1][0])
    own.append(attend_here(gate, query[-1], near[-1], far[-1]))
    last_hop = after(handed[2], own[-1][0])
    late = lax.ppermute(after(part1[count - 2], last_hop)[size:], "seq", [(4, 6), (5, 7)])
    before = jnp.where(chip == 1, handed[0], jnp.where(chip == 2, handed[1], jnp.where(chip == 3, last_hop, 0)))
    other = lax.ppermute(before, "seq", swap)
    before = jnp.where(core == 0, jnp.concatenate([before, other]), jnp.concatenate([other, before]))
    mixed, squares = mix(after(gate, own[-1][0]), lin_q, lin_k, lin_v, before, sib_states)

    def complete(which, *behind):
        chunks, spans = [], []
        for i in which:
            other = part2 if i == count - 1 else late if i == count - 2 else passed
            spans.append((0, i * size if i < count - 2 else 0))
            chunks.append((own[i][1], part1[i], other, own[i][0]))
        return finish(after(place, *behind), chunks, tuple(spans), FINISH_US if which[0] == count - 1 else SERVE_US)

    keep, give = complete(list(range(count - 1)), mixed)
    squares = squares + lax.ppermute(squares, "grp", [(0, 1), (1, 0), (2, 3), (3, 2)])
    squares = after(squares, keep)
    squares = squares + lax.ppermute(squares, "grp", [(0, 2), (2, 0), (1, 3), (3, 1)])
    keep_last, give_last = complete([count - 1])
    got = lax.ppermute(jnp.concatenate([give, give_last], axis=1), "seq", swap)
    inverse = lax.rsqrt(after(squares, keep_last)[:, :1] / (HEADS * HEAD_DIM) + epsilon)
    lin_out = (mixed * inverse * lin_gain).astype(BF16)
    here, there = [keep, keep_last], [got]
    soft_out = jnp.where(core == 0, jnp.concatenate(here + there, axis=1), jnp.concatenate(there + here, axis=1))
    return (lin_out, soft_out)


def shards(*arrays):
    heads = arrays[0].shape[1] // HEAD_DIM
    if lax.axis_size("seq") == 8 and lax.axis_size("grp") == 4 and heads == 2 * sum(CHUNKS):
        return line_of_four(*arrays)
    return any_ring(*arrays)


def solution(mesh):
    return jax.shard_map(
        shards,
        mesh=mesh,
        in_specs=(
            P("seq", "grp"),
            P("seq", "grp"),
            P("seq", "grp"),
            P("grp"),
            P("seq", "grp"),
            P("seq", "grp"),
            P("seq", "grp"),
        ),
        out_specs=(P("seq", "grp"), P("seq", "grp")),
        check_vma=False,
    )
```

```python
import functools

import jax
import jax.numpy as jnp
from jax import lax
from jax.experimental import pallas as pl
from jax.experimental.pallas import tpu as pltpu
from jax.sharding import PartitionSpec as P

HEADS = 64
HEAD_DIM = 128
LSE_ROWS = 16
OPEN_ROWS = 8
PAD_ROWS = 16
CHUNKS = (2, 2, 2, 2)
STEP = 4
SERVE_US = 0.001
LAST_US = 0.001
FINISH_US = 30.0
OWN_US = 0.001
VMEM = 8 * 1024 * 1024

highest = lax.Precision.HIGHEST
epsilon = 1e-06
F32 = jnp.float32
BF16 = jnp.bfloat16
LOG2 = HEAD_DIM ** (-0.5) * 1.4426950408889634
NT = (((1,), (1,)), ((), ()))
TN = (((0,), (0,)), ((), ()))


def dot_nt(a, b):
    return lax.dot_general(a, b, NT, preferred_element_type=F32)


def dot_tn(a, b):
    return lax.dot_general(a, b, TN, preferred_element_type=F32)


def dot(a, b):
    return jnp.dot(a, b, preferred_element_type=F32)


def split(a):
    high = a.astype(BF16)
    return high, (a - high.astype(F32)).astype(BF16)


def after(value, *others):
    return lax.optimization_barrier((value, *others))[0]


def causal_mask(rows):
    row_ids = lax.broadcasted_iota(jnp.int32, (rows, rows), 0)
    col_ids = lax.broadcasted_iota(jnp.int32, (rows, rows), 1)
    return col_ids <= row_ids


def lanes(ref, head):
    return ref[:, head * HEAD_DIM : (head + 1) * HEAD_DIM]


def weigh(scores, values, top):
    both = None
    for score, value in zip(scores, values):
        weights = jnp.exp2(score * LOG2 - top).astype(BF16)
        part = dot(weights, jnp.concatenate([value, jnp.ones_like(value)], axis=1))
        both = part if both is None else both + part
    return both[:, :HEAD_DIM], both[:, HEAD_DIM:]


def attend(query, keys, values, mask=None):
    scores = [dot_nt(query, key) for key in keys]
    if mask is not None:
        scores[-1] = jnp.where(mask, scores[-1], -1e30)
    top = jnp.max(functools.reduce(jnp.maximum, scores), axis=1, keepdims=True) * LOG2
    numerator, total = weigh(scores, values, top)
    return numerator * (1.0 / total), top + jnp.log2(total)


def level_rows(level, tile, pieces):
    rows = level.shape[0]
    across = jnp.transpose(level)[:1]
    parts = []
    for _ in range(pieces):
        part = across if pieces == 1 else across.astype(BF16).astype(F32)
        across = across - part
        parts += [part[:, i : i + HEAD_DIM] for i in range(0, rows, HEAD_DIM)]
    parts.append(jnp.zeros((tile - len(parts), HEAD_DIM), F32))
    return jnp.concatenate(parts, axis=0)


def read_level(packed, rows, pieces):
    halves = rows // HEAD_DIM
    level = packed.astype(F32)
    columns = []
    for i in range(halves):
        line = sum(level[j * halves + i : j * halves + i + 1] for j in range(pieces))
        columns.append(jnp.transpose(jnp.broadcast_to(line, (HEAD_DIM, HEAD_DIM))))
    return jnp.concatenate(columns, axis=0)


def blocks_of(ref, head, rows):
    both = lanes(ref, head)
    return [both[i : i + rows] for i in range(0, ref.shape[0], rows)]


def across(head):
    return slice(head * HEAD_DIM, (head + 1) * HEAD_DIM)


def gather(refs, head, rows):
    blocks = [blocks_of(ref, head, rows) for ref in refs]
    return sum((b[:2] for b in blocks), []), sum((b[2:] for b in blocks), [])


def run(copies):
    for copy in copies:
        copy.start()
    for copy in copies:
        copy.wait()


def serve_kernel(together, place, first_hbm, second_hbm, near_hbm, far_hbm, *rest):
    sent_hbm, (first_ref, second_ref, near_ref, far_ref, sent_ref, sems) = rest[:-6], rest[-6:]
    pair, width = near_ref.shape[0] // 2, near_ref.shape[1]
    rows = pair // 2
    size = pair + 2 * LSE_ROWS
    answers = [sent_hbm[0].at[pl.ds(0, size)], sent_hbm[0].at[pl.ds(size, size)]] if together else sent_hbm

    def copies(pairs):
        return [pltpu.make_async_copy(src, dst, sems.at[i]) for i, (src, dst) in enumerate(pairs)]

    @pl.when(place[0] == 1)
    def _():
        run(copies([(near_hbm, near_ref), (far_hbm, far_ref), (first_hbm, first_ref), (second_hbm, second_ref)]))
        if not together:
            sent_ref[:, size:] = jnp.zeros_like(sent_ref[:, size:])
        for head in range(width // HEAD_DIM):
            keys, values = gather([near_ref, far_ref], head, rows)
            for slot, query_ref in enumerate([first_ref, second_ref]):
                for i in range(2):
                    part, level = attend(query_ref[i * rows : (i + 1) * rows, across(head)], keys, values)
                    sent_ref[slot, i * rows : (i + 1) * rows, across(head)] = part.astype(BF16)
                    there = slice(pair + i * LSE_ROWS, pair + (i + 1) * LSE_ROWS)
                    sent_ref[slot, there, across(head)] = level_rows(level, LSE_ROWS, 3).astype(BF16)
        run(copies([(sent_ref.at[0], answers[0]), (sent_ref.at[1], answers[1])]))


def own_kernel(place, query_hbm, near_hbm, far_hbm, closed_hbm, open_hbm, query_ref, near_ref, far_ref, closed_ref, open_ref, sems):
    pair, width = near_ref.shape[0] // 2, near_ref.shape[1]
    rows = pair // 2
    chip = place[0]
    mask = causal_mask(rows)

    def copies(pairs):
        return [pltpu.make_async_copy(src, dst, sems.at[i]) for i, (src, dst) in enumerate(pairs)]

    def attend_own(refs, closed):
        for head in range(width // HEAD_DIM):
            near = blocks_of(near_ref, head, rows)
            keys, values = gather(refs, head, rows)
            for i in range(2):
                here = slice(i * rows, (i + 1) * rows)
                part, level = attend(query_ref[here, across(head)], keys + near[: i + 1], values + near[2 : 3 + i], mask)
                if closed:
                    closed_ref[here, across(head)] = part.astype(BF16)
                else:
                    open_ref[here, across(head)] = part
                    there = slice(pair + i * OPEN_ROWS, pair + (i + 1) * OPEN_ROWS)
                    open_ref[there, across(head)] = level_rows(level, OPEN_ROWS, 1)

    fetch = [(near_hbm, near_ref), (query_hbm, query_ref)]

    @pl.when(chip == 0)
    def _():
        run(copies(fetch))
        attend_own([], True)
        run(copies([(closed_ref, closed_hbm)]))

    @pl.when(chip == 1)
    def _():
        run(copies(fetch + [(far_hbm, far_ref)]))
        attend_own([far_ref], True)
        run(copies([(closed_ref, closed_hbm)]))

    @pl.when(chip == 2)
    def _():
        run(copies(fetch))
        attend_own([], False)
        run(copies([(open_ref, open_hbm)]))

    @pl.when(chip == 3)
    def _():
        run(copies(fetch + [(far_hbm, far_ref)]))
        attend_own([far_ref], False)
        run(copies([(open_ref, open_hbm)]))


def finish_kernel(spans, place, *refs):
    count = len(spans)
    inputs, (keep_hbm, give_hbm, open_ref, part_ref, out_ref, sems) = refs[: 4 * count], refs[4 * count :]
    rows = keep_hbm.shape[0]
    pair, width = 2 * rows, out_ref.shape[2]
    size = pair + 2 * LSE_ROWS
    chip, core = place[0], place[1]

    def hand_out():
        def copies(early_hbm, late_hbm):
            moves = []
            for c in range(count):
                for half, target in enumerate((early_hbm, late_hbm)):
                    there = target.at[:, pl.ds(c * width, width)]
                    moves.append(pltpu.make_async_copy(out_ref.at[c, pl.ds(half * rows, rows)], there, sems.at[2 * c + half]))
            run(moves)

        @pl.when(core == 0)
        def _():
            copies(keep_hbm, give_hbm)

        @pl.when(core == 1)
        def _():
            copies(give_hbm, keep_hbm)

    def merge(which):
        fetch = []
        for c, starts in enumerate(spans):
            moves = [
                pltpu.make_async_copy(inputs[4 * c], open_ref.at[c], sems.at[2 * c]),
                pltpu.make_async_copy(inputs[4 * c + which].at[pl.ds(starts[which - 1], size)], part_ref.at[c], sems.at[2 * c + 1]),
            ]
            for move in moves:
                move.start()
            fetch.append(moves)
        for c in range(count):
            for move in fetch[c]:
                move.wait()
            for head in range(width // HEAD_DIM):
                lane = across(head)
                for i in range(2):
                    here = slice(i * rows, (i + 1) * rows)
                    there = slice(pair + i * OPEN_ROWS, pair + (i + 1) * OPEN_ROWS)
                    terms = [(open_ref[c, here, lane], read_level(open_ref[c, there, lane], rows, 1))]
                    there = slice(pair + i * LSE_ROWS, pair + (i + 1) * LSE_ROWS)
                    terms.append((part_ref[c, here, lane].astype(F32), read_level(part_ref[c, there, lane], rows, 3)))
                    top = functools.reduce(jnp.maximum, [level for _, level in terms])
                    weights = [jnp.exp2(level - top) for _, level in terms]
                    mixed = sum(weight * part for weight, (part, _) in zip(weights, terms))
                    out_ref[c, here, lane] = (mixed * (1.0 / sum(weights))).astype(BF16)
        hand_out()

    @pl.when(chip <= 1)
    def _():
        run([pltpu.make_async_copy(inputs[4 * c + 3], out_ref.at[c], sems.at[c]) for c in range(count)])
        hand_out()

    @pl.when(chip == 2)
    def _():
        merge(1)

    @pl.when(chip == 3)
    def _():
        merge(2)


def col_block(rows, step, offset=0):
    return pl.BlockSpec((rows, step * HEAD_DIM), lambda h: (0, offset // step + h))


SMEM_SPEC = pl.BlockSpec(memory_space=pltpu.SMEM)
ANY_SPEC = pl.BlockSpec(memory_space=pl.ANY)
HBM_SPEC = pl.BlockSpec(memory_space=pltpu.HBM)
STATE_SPEC = pl.BlockSpec((STEP // 2 * HEAD_DIM, 2 * HEAD_DIM), lambda h: (h, 0))
VMEM_SPEC = pl.BlockSpec(memory_space=pltpu.VMEM)


def params():
    return pltpu.CompilerParams(vmem_limit_bytes=VMEM)


def cost(microseconds):
    return pl.CostEstimate(flops=int(microseconds * 1.1e9), bytes_accessed=1, transcendentals=0)


def tiny():
    return pl.CostEstimate(flops=1, bytes_accessed=1, transcendentals=0)


def serve(place, first, second, near, far, together, microseconds):
    pair, width = near.shape[0] // 2, near.shape[1]
    size = pair + 2 * LSE_ROWS + (0 if together else PAD_ROWS)
    sent = [(2 * size, width)] if together else [(size, width)] * 2
    return pl.pallas_call(
        functools.partial(serve_kernel, together),
        out_shape=[jax.ShapeDtypeStruct(x, BF16) for x in sent],
        in_specs=[SMEM_SPEC] + [ANY_SPEC] * 4,
        out_specs=[ANY_SPEC] * len(sent),
        scratch_shapes=[pltpu.VMEM(x.shape, BF16) for x in (first, second, near, far)]
        + [pltpu.VMEM((2, size, width), BF16), pltpu.SemaphoreType.DMA((4,))],
        compiler_params=params(),
        cost_estimate=cost(microseconds),
        name="serve",
    )(place, first, second, near, far)


def attend_here(place, query, near, far):
    closed = (near.shape[0] // 2, near.shape[1])
    opened = (closed[0] + 2 * OPEN_ROWS, closed[1])
    return pl.pallas_call(
        own_kernel,
        out_shape=[jax.ShapeDtypeStruct(closed, BF16), jax.ShapeDtypeStruct(opened, F32)],
        in_specs=[SMEM_SPEC] + [ANY_SPEC] * 3,
        out_specs=[HBM_SPEC] * 2,
        scratch_shapes=[pltpu.VMEM(x, BF16) for x in (query.shape, near.shape, far.shape, closed)]
        + [pltpu.VMEM(opened, F32), pltpu.SemaphoreType.DMA((3,))],
        compiler_params=params(),
        cost_estimate=cost(OWN_US),
        name="own",
    )(place, query, near, far)


def finish(place, chunks, spans, microseconds):
    count = len(chunks)
    pair, width = chunks[0][3].shape
    out = jax.ShapeDtypeStruct((pair // 2, count * width), BF16)
    part = (count, pair + 2 * LSE_ROWS, width)
    return pl.pallas_call(
        functools.partial(finish_kernel, spans),
        out_shape=(out, out),
        in_specs=[SMEM_SPEC] + [HBM_SPEC] * (4 * count),
        out_specs=(ANY_SPEC, ANY_SPEC),
        scratch_shapes=[
            pltpu.VMEM((count, *chunks[0][0].shape), F32),
            pltpu.VMEM(part, BF16),
            pltpu.VMEM((count, pair, width), BF16),
            pltpu.SemaphoreType.DMA((2 * count,)),
        ],
        compiler_params=params(),
        cost_estimate=cost(microseconds),
        name="finish",
    )(place, *[x for chunk in chunks for x in chunk])


def state_place(head):
    return slice(head // 2 * HEAD_DIM, (head // 2 + 1) * HEAD_DIM), slice(head % 2 * HEAD_DIM, (head % 2 + 1) * HEAD_DIM)


def state_kernel(key_ref, value_ref, state_ref):
    for head in range(STEP):
        state_ref[state_place(head)] = dot_tn(lanes(key_ref, head), lanes(value_ref, head))


def own_states(keys, values):
    rows, width = keys.shape
    heads = width // HEAD_DIM
    return pl.pallas_call(
        state_kernel,
        grid=(heads // STEP,),
        out_shape=jax.ShapeDtypeStruct((heads // 2 * HEAD_DIM, 2 * HEAD_DIM), F32),
        in_specs=[col_block(rows, STEP), col_block(rows, STEP)],
        out_specs=STATE_SPEC,
        compiler_params=params(),
        cost_estimate=cost(1.0),
        name="states",
    )(keys, values)


def mix_kernel(place, query_ref, key_ref, value_ref, before_ref, sib_ref, mixed_ref, square_ref):
    rows, width = query_ref.shape
    mask = causal_mask(rows)
    squares = jnp.zeros((rows, HEAD_DIM), F32)
    for head in range(width // HEAD_DIM):
        query, value = lanes(query_ref, head), lanes(value_ref, head)
        high, low = split(jnp.where(mask, dot_nt(query, lanes(key_ref, head)), 0.0))
        state = state_place(head)
        prefix = before_ref[state].astype(F32) + jnp.where(place[1] == 1, sib_ref[state], 0.0)
        prefix_high, prefix_low = split(prefix)
        mixed = dot(high, value) + dot(low, value) + dot(query, prefix_high) + dot(query, prefix_low)
        mixed_ref[:, head * HEAD_DIM : (head + 1) * HEAD_DIM] = mixed
        squares = squares + mixed * mixed

    @pl.when(pl.program_id(0) == 0)
    def _():
        square_ref[...] = squares

    @pl.when(pl.program_id(0) > 0)
    def _():
        square_ref[...] += squares

    @pl.when(pl.program_id(0) == pl.num_programs(0) - 1)
    def _():
        square_ref[...] = jnp.broadcast_to(jnp.sum(square_ref[...], axis=1, keepdims=True), square_ref.shape)


def mix(place, queries, keys, values, before, sib_state):
    rows, width = keys.shape
    heads = width // HEAD_DIM
    return pl.pallas_call(
        mix_kernel,
        grid=(heads // STEP,),
        out_shape=(jax.ShapeDtypeStruct((rows, width), F32), jax.ShapeDtypeStruct((rows, HEAD_DIM), F32)),
        in_specs=[SMEM_SPEC, col_block(rows, STEP), col_block(rows, STEP), col_block(rows, STEP), STATE_SPEC, STATE_SPEC],
        out_specs=(col_block(rows, STEP), pl.BlockSpec((rows, HEAD_DIM), lambda h: (0, 0))),
        compiler_params=params(),
        cost_estimate=tiny(),
        name="mix",
    )(place, queries, keys, values, before, sib_state)


def from_behind(value, axis, by):
    peers = lax.axis_size(axis)
    pairs = [(i, i + by) for i in range(peers) if 0 <= i + by < peers]
    return lax.ppermute(value, axis, pairs)


def any_ring(lin_q, lin_k, lin_v, lin_gain, soft_q, soft_k, soft_v):
    rows_dev, width_dev = lin_q.shape
    head_size = HEAD_DIM
    local_heads = width_dev // head_size
    queries_low = lin_q.reshape(rows_dev, local_heads, head_size)
    keys_low = lin_k.reshape(rows_dev, local_heads, head_size)
    values_low = lin_v.reshape(rows_dev, local_heads, head_size)
    queries = queries_low.astype(jnp.float32)
    values_lin = values_low.astype(jnp.float32)
    own_state = jnp.einsum("thd,the->hde", keys_low, values_low, preferred_element_type=jnp.float32)
    zero_state = jnp.zeros_like(own_state)

    def relay_step(counter, running):
        return from_behind(running + own_state, "seq", 1)

    prefix = lax.fori_loop(0, lax.axis_size("seq") - 1, relay_step, zero_state)
    row_ids = lax.broadcasted_iota(jnp.int32, (rows_dev, rows_dev), 0)
    col_ids = lax.broadcasted_iota(jnp.int32, (rows_dev, rows_dev), 1)
    causal = (col_ids <= row_ids).astype(jnp.float32)
    scores_lin = (
        jnp.einsum("thd,shd->hts", queries_low, keys_low, preferred_element_type=jnp.float32)
        * causal[None]
    )
    within = jnp.einsum("hts,she->the", scores_lin, values_lin, precision=highest)
    carried = jnp.einsum("thd,hde->the", queries, prefix, precision=highest)
    mixed_out = (within + carried).reshape(rows_dev, width_dev)
    squares = jnp.sum(mixed_out * mixed_out, axis=1)
    summed = lax.psum(squares, "grp")
    inverse = lax.rsqrt(summed / (HEADS * head_size) + epsilon)
    lin_out = (mixed_out * inverse[:, None] * lin_gain).astype(jnp.bfloat16)
    seq_devices = lax.axis_size("seq")
    seq_index = lax.axis_index("seq")
    units = 2 * local_heads // seq_devices
    half_rows = rows_dev // 2
    query_units = (
        soft_q.reshape(2, half_rows, local_heads, head_size)
        .transpose(2, 0, 1, 3)
        .reshape(2 * local_heads, half_rows, head_size)
    )

    def head_pieces(source):
        shaped = source.reshape(rows_dev, local_heads, head_size)
        if units == 1:
            shaped = jnp.repeat(shaped, 2, axis=1)
        return shaped.transpose(1, 0, 2)

    query_in, keys_in, values_in = (
        lax.all_to_all(query_units, "seq", split_axis=0, concat_axis=1, tiled=True),
        lax.all_to_all(head_pieces(soft_k), "seq", split_axis=0, concat_axis=1, tiled=True),
        lax.all_to_all(head_pieces(soft_v), "seq", split_axis=0, concat_axis=1, tiled=True),
    )
    seq_len = seq_devices * rows_dev
    query_rows = seq_len // 2
    block_rows = query_rows // 8
    scale = head_size ** (-0.5)
    outputs = []
    for unit_index in range(units):
        half_index = (seq_index * units + unit_index) % 2
        head_slot = unit_index // 2
        pieces = []
        for block_index in range(8):
            key_count = (block_index + 1) * seq_len // 8
            block_q = query_in[
                unit_index, block_index * block_rows : (block_index + 1) * block_rows
            ]
            block_k = keys_in[head_slot, :key_count]
            block_v = values_in[head_slot, :key_count]
            scores = (
                jnp.einsum("qd,kd->qk", block_q, block_k, preferred_element_type=jnp.float32)
                * scale
            )
            local_rows = block_index * block_rows + lax.broadcasted_iota(
                jnp.int32, (block_rows, 1), 0
            )
            positions_q = (
                local_rows // half_rows * rows_dev + half_index * half_rows + local_rows % half_rows
            )
            positions_k = lax.broadcasted_iota(jnp.int32, (1, key_count), 1)
            scores = jnp.where(positions_k <= positions_q, scores, -1e30)
            largest = jnp.max(scores, axis=1, keepdims=True)
            exponent = jnp.exp(scores - largest)
            denominator = jnp.sum(exponent, axis=1, keepdims=True)
            weights = exponent.astype(jnp.bfloat16)
            numerator = jnp.dot(weights, block_v, preferred_element_type=jnp.float32)
            pieces.append((numerator / denominator).astype(jnp.bfloat16))
        outputs.append(jnp.concatenate(pieces, axis=0))
    unit_out = jnp.stack(outputs, axis=0)
    returned = lax.all_to_all(unit_out, "seq", split_axis=1, concat_axis=0, tiled=True)
    soft_out = (
        returned.reshape(local_heads, 2, half_rows, head_size)
        .transpose(1, 2, 0, 3)
        .reshape(rows_dev, width_dev)
    )
    return (lin_out, soft_out)


def line_of_four(lin_q, lin_k, lin_v, lin_gain, soft_q, soft_k, soft_v):
    rows, width = lin_q.shape
    half = width // 2
    index = lax.axis_index("seq")
    core = index % 2
    place = jnp.stack([index // 2, core]).astype(jnp.int32)
    swap = [(i, i ^ 1) for i in range(8)]
    up = [(i, i + 1) for i in range(0, 8, 2)]
    down = [(i + 1, i) for i in range(0, 8, 2)]
    count = len(CHUNKS)
    offsets = [sum(CHUNKS[:i]) for i in range(count)]
    columns = [slice(o * HEAD_DIM, (o + c) * HEAD_DIM) for o, c in zip(offsets, CHUNKS)]

    chip = place[0]

    chip = place[0]

    def prologue():
        here = columns[0]
        there = slice(here.start + half, here.stop + half)
        keep = [jnp.where(core == 0, x[:, here], x[:, there]) for x in (soft_k, soft_v, soft_q)]
        give = jnp.concatenate([jnp.where(core == 0, x[:, there], x[:, here]) for x in (soft_k, soft_v, soft_q)], axis=0)
        got = lax.ppermute(give, "seq", swap)
        both = [(x, got[i * rows : (i + 1) * rows]) for i, x in enumerate(keep)]
        ordered = [jnp.where(core == 0, jnp.concatenate([x, y]), jnp.concatenate([y, x])) for x, y in both]
        return jnp.concatenate(ordered[:2], axis=0), ordered[2]

    def chunk(sources, i):
        here, there = columns[i], slice(columns[i].start + half, columns[i].stop + half)
        low = [x[:, here] for pair in sources for x in pair]
        high = [x[:, there] for pair in sources for x in pair[::-1]]
        return jnp.concatenate([jnp.where(core == 0, x, y) for x, y in zip(low, high)], axis=0)

    first, second, far, query, near = [], [], [], [], []

    def send(i, *behind):
        far.append(lax.ppermute(after(near[i], *behind), "seq", [(0, 2), (1, 3), (4, 6), (5, 7)]))
        source = after(query[i], *behind)
        first.append(lax.ppermute(source, "seq", [(4, 2), (5, 3)]))
        second.append(lax.ppermute(source, "seq", [(6, 2), (7, 3)]))

    near_0, query_0 = prologue()
    near.append(near_0)
    query.append(jnp.pad(query_0, ((0, PAD_ROWS), (0, 0))))
    send(0)
    keys, values, queries = [(x, lax.ppermute(after(x, near_0), "seq", swap)) for x in (soft_k, soft_v, soft_q)]
    states = own_states(after(lin_k, query_0), lin_v)
    sib_states = lax.ppermute(states, "seq", swap)
    for i in range(1, count):
        near.append(chunk([keys, values], i))
        query.append(jnp.pad(chunk([queries], i), ((0, PAD_ROWS), (0, 0))))
    state_rows = states.shape[0] // 2
    chip_states = lax.dynamic_slice_in_dim(states + sib_states, core * state_rows, state_rows, axis=0)
    handed = []

    def hop(*behind):
        i = len(handed)
        running = chip_states + handed[-1].astype(F32) if handed else chip_states
        running = after(running.astype(BF16), *behind)
        if i == 2:
            running = jnp.pad(running, ((0, state_rows // 2), (0, 0)))
        sent = lax.ppermute(running, "seq", [(2 * i, 2 * i + 2), (2 * i + 1, 2 * i + 3)])
        handed.append(sent[:state_rows])

    hop()
    size = 2 * rows + 2 * LSE_ROWS
    part1, part2, served, own = [], [], [], []
    waits = [*near, *query]
    for i in range(count):
        if i >= 2:
            waits.append(part1[i - 2])
        gate = after(place, first[i], second[i], far[i])
        gate = after(gate, *waits)
        waits = []
        if i + 1 < count:
            send(i + 1, gate)
        if i == count - 1:
            hop(gate)
            waits.append(handed[-1])
        final = i == count - 1
        if final:
            passed = jnp.concatenate([x[size:] for x in part1[:i - 1]], axis=0)
            passed = lax.ppermute(after(passed, gate), "seq", [(4, 6), (5, 7)])
        served.append(serve(gate, first[i], second[i], near[i], far[i], not final, LAST_US if final else SERVE_US))
        part1.append(lax.ppermute(served[-1][0], "seq", [(2, 4), (3, 5)]))
        if final:
            part2 = lax.ppermute(served[-1][1], "seq", [(2, 6), (3, 7)])
        else:
            own.append(attend_here(after(place, served[-1][0]), query[i], near[i], far[i]))
            waits.append(own[-1][0])
            if i == 0:
                hop(own[-1][0])
                waits.append(handed[-1])
    gate = after(place, served[-1][0])
    own.append(attend_here(gate, query[-1], near[-1], far[-1]))
    last_hop = after(handed[2], own[-1][0])
    late = lax.ppermute(after(part1[count - 2], last_hop)[size:], "seq", [(4, 6), (5, 7)])
    before = jnp.where(chip == 1, handed[0], jnp.where(chip == 2, handed[1], jnp.where(chip == 3, last_hop, 0)))
    other = lax.ppermute(before, "seq", swap)
    before = jnp.where(core == 0, jnp.concatenate([before, other]), jnp.concatenate([other, before]))
    mixed, squares = mix(after(gate, own[-1][0]), lin_q, lin_k, lin_v, before, sib_states)

    def complete(which, *behind):
        chunks, spans = [], []
        for i in which:
            other = part2 if i == count - 1 else late if i == count - 2 else passed
            spans.append((0, i * size if i < count - 2 else 0))
            chunks.append((own[i][1], part1[i], other, own[i][0]))
        return finish(after(place, *behind), chunks, tuple(spans), FINISH_US if which[0] == count - 1 else SERVE_US)

    keep, give = complete(list(range(count - 1)), mixed)
    squares = squares + lax.ppermute(squares, "grp", [(0, 1), (1, 0), (2, 3), (3, 2)])
    squares = squares + lax.ppermute(squares, "grp", [(0, 2), (2, 0), (1, 3), (3, 1)])
    keep_last, give_last = complete([count - 1])
    got = lax.ppermute(jnp.concatenate([give, give_last], axis=1), "seq", swap)
    inverse = lax.rsqrt(squares[:, :1] / (HEADS * HEAD_DIM) + epsilon)
    lin_out = (mixed * inverse * lin_gain).astype(BF16)
    here, there = [keep, keep_last], [got]
    soft_out = jnp.where(core == 0, jnp.concatenate(here + there, axis=1), jnp.concatenate(there + here, axis=1))
    return (lin_out, soft_out)


def shards(*arrays):
    heads = arrays[0].shape[1] // HEAD_DIM
    if lax.axis_size("seq") == 8 and lax.axis_size("grp") == 4 and heads == 2 * sum(CHUNKS):
        return line_of_four(*arrays)
    return any_ring(*arrays)


def solution(mesh):
    return jax.shard_map(
        shards,
        mesh=mesh,
        in_specs=(
            P("seq", "grp"),
            P("seq", "grp"),
            P("seq", "grp"),
            P("grp"),
            P("seq", "grp"),
            P("seq", "grp"),
            P("seq", "grp"),
        ),
        out_specs=(P("seq", "grp"), P("seq", "grp")),
        check_vma=False,
    )
```
